32 devices in a mesh: ctx: 4 (over z), enc: 4 (over y, core), mp: 2 (over x).
Axes of the slice: x: 2, y: 2, z: 4, core: 2. Of those that a mesh axis runs over, the one named last changes fastest.
Arguments:
- hidden_in: bfloat16 [1024, 4096], P('ctx'), may hold values from -6 to 6
- norm_gains: float32 [2, 4096], replicated, may hold values from 0.5 to 1.5
- w_cross_query: bfloat16 [4096, 2048], P('ctx', ('enc', 'mp')), may hold values from -1 to 1
- w_cross_out: bfloat16 [2048, 4096], P(('enc', 'mp'), 'ctx'), may hold values from -0.125 to 0.125
- w_self_qkv: bfloat16 [4096, 3, 2048], P('ctx', None, ('enc', 'mp')), may hold values from -1 to 1
- w_self_out: bfloat16 [2048, 4096], P(('enc', 'mp'), 'ctx'), may hold values from -0.125 to 0.125
- nbr_kv: bfloat16 [4, 4, 4, 3, 64, 1024], P('ctx', 'enc', None, None, None, 'mp'), may hold values from -6 to 6
- nbr_count: int32 [16], P('ctx'), may hold values from 1 to 2
- nbr_source: int32 [16, 2], P('ctx'), may hold values from 0 to 3, all different within a row; in each aligned block of 4 rows (0 to 3, 4 to 7, ...) at most 3 rows name the same one
- span_order: int32 [16], replicated, may hold values from 0 to 15, each once
Outputs:
- block_out: bfloat16 [1024, 4096], P('ctx', ('enc', 'mp'))
The draws below stay inside these ranges and needn't reach their ends.
Inputs may be any that keep to these rules, and one draw needn't show every extreme that they name: `nbr_source`: within the 4 stored spans of one index of ctx (aligned blocks of rows), no encoder index is named more than 3 times, and one is named exactly 3 times in some block; the 2 entries of a span differ. `span_order`: each of the 16 positions appears once.
All inputs are finite; a program needn't handle non-finite values.
Results may differ from the reference program's by a relative error of at most 0.015.
Values may be sent and summed in bfloat16 or wider, within the bound.
A program may use at most 128 MiB of HBM per device.

```python
import math
import jax
import jax.numpy as jnp
import numpy as np
from jax import lax

D = 4096
HEADS = 16
HD = 128
SPAN = 64
NBR = 2
NBR_ROWS = 64
CH_DEV = 4
CAP = 3
SPANS = 16
SEQ = 1024
N_CTX = 4
N_ENC = 4
N_MP = 2


def draw_hidden_in(key, part):
    own_key = jax.random.fold_in(key, 11)
    values = jax.random.truncated_normal(own_key, -6.0, 6.0, (SEQ, D), jnp.float32)
    return values.astype(jnp.bfloat16)


def draw_w_cross_query(key, part):
    own_key = jax.random.fold_in(key, 12)
    values = jax.random.truncated_normal(own_key, -6.0, 6.0, (D, HEADS * HD), jnp.float32) / math.sqrt(D)
    return values.astype(jnp.bfloat16)


def draw_w_self_qkv(key, part):
    own_key = jax.random.fold_in(key, 13)
    values = jax.random.truncated_normal(own_key, -6.0, 6.0, (D, 3, HEADS * HD), jnp.float32) / math.sqrt(D)
    return values.astype(jnp.bfloat16)


def draw_nbr_kv(key, part):
    own_key = jax.random.fold_in(key, 14)
    per_group = HEADS // N_ENC
    values = jax.random.truncated_normal(own_key, -6.0, 6.0, (N_CTX, N_ENC, N_ENC, CAP, NBR_ROWS, per_group, 2, HD), jnp.float32)
    values = values.reshape(N_CTX, N_ENC, N_ENC, CAP, NBR_ROWS, per_group * 2 * HD)
    return values.astype(jnp.bfloat16)


def set_ends(entries, rng, least, high):
    shape = entries.shape
    place = [jax.random.randint(jax.random.fold_in(rng, axis), (), 0, shape[axis]) for axis in range(len(shape))]
    entries = entries.at[tuple(place)].set(least)
    longest = shape.index(max(shape))
    place[longest] = (place[longest] + 1) % shape[longest]
    return entries.at[tuple(place)].set(high)


def levels(key, shape, cuts, least, largest):
    def one(position, blocks):
        steps = jax.random.uniform(jax.random.fold_in(jax.random.fold_in(key, 6), position), (blocks,), jnp.float32, least / len(cuts), largest / len(cuts))
        return jnp.repeat(jnp.exp(steps), shape[position] // blocks).reshape((-1,) + (1,) * (len(shape) - position - 1))

    level = one(*cuts[0])
    for cut in cuts[1:]:
        level = level * one(*cut)
    return level


def assign_block(rng, own, number, rows, amount, top, reach, lean):
    sequence = jax.random.permutation(rng, amount)
    heavy_load, usual = portions_of(amount, rows * top, reach, lean, True), portions_of(amount, rows * top, reach, lean, False)
    places = jnp.arange(amount)

    def named(tallies, rotation):
        used = int((tallies > 0).sum())
        fixed = max(1, used // 4)
        shifted = fixed + (places - fixed + rotation * (used - fixed)) % max(1, amount - fixed)
        return jnp.zeros((amount,), jnp.int32).at[sequence[jnp.where(places < fixed, places, shifted)]].set(jnp.asarray(tallies, jnp.int32))

    tallies = jnp.where(number % 4 == 0, named(heavy_load, number // 4), named(usual, number - number // 4 - 1))
    mixed = jax.random.permutation(jax.random.fold_in(own, 3), amount)
    source_of, sink = mixed[0:amount // 2 * 2:2], mixed[1:amount // 2 * 2:2]
    margin = jnp.minimum(tallies[source_of] - 1, reach - tallies[sink]) // 2
    margin = jnp.where((source_of == sequence[0]) | (sink == sequence[0]) | (tallies[sink] == 0), 0, jnp.maximum(margin, 0))
    shifted = jax.random.randint(jax.random.fold_in(own, 4), (amount // 2,), 0, 1 << 20) % (margin + 1)
    tallies = tallies.at[source_of].add(-shifted).at[sink].add(shifted)
    items = jnp.searchsorted(jnp.cumsum(tallies), jnp.arange(rows * top), side="right").astype(jnp.int32)
    table = items.reshape(top, rows).T
    table = table[jax.random.permutation(jax.random.fold_in(own, 1), rows)]
    rotation = jax.random.randint(jax.random.fold_in(own, 2), (rows, 1), 0, top)
    return jnp.take_along_axis(table, (jnp.arange(top)[None, :] + rotation) % top, axis=1)


def portions_of(amount, total, most, skew, full):
    loads = [(1 << 20) // math.isqrt(standing ** skew) + 1 for standing in range(1, amount + 1)]
    largest = most if full else min(most, max(-(-total // amount), total * loads[0] // sum(loads)))
    least = 1 if total - largest >= amount - 1 else 0
    holding, surplus = [largest] + [least] * (amount - 1), total - largest - least * (amount - 1)
    while surplus > 0:
        movable = [i for i in range(1, amount) if holding[i] < largest] or [i for i in range(1, amount) if holding[i] < most]
        pool, budget = sum([loads[i] for i in movable]), surplus
        for i in movable:
            extra = min(most - holding[i], max(1, budget * loads[i] // pool), surplus)
            holding[i] = holding[i] + extra
            surplus = surplus - extra
    return np.array(holding)


def noise(key, shape, spread, reach, pieces=(), kind=jnp.bfloat16):
    drawn = spread * jax.random.normal(key, shape, jnp.float32)
    if pieces:
        drawn = drawn * levels(key, shape, pieces, -0.22, 0.18)
    return jnp.clip(drawn, -reach, reach).astype(kind)


def setup_inputs(seed: int = 0) -> dict:
    streams_of = jax.random.split(jax.random.key(seed), 11)
    hidden_in = draw_hidden_in(jax.random.fold_in(streams_of[10], 71), 0)
    norm_gains = jnp.clip(1.0 + 0.1 * jax.random.normal(streams_of[1], (2, D), jnp.float32), 0.5, 1.5)
    w_cross_query = draw_w_cross_query(jax.random.fold_in(streams_of[10], 71), 0)
    w_cross_out = noise(streams_of[3], (HEADS * HD, D), (HEADS * HD) ** -0.5, 0.125, ((0, 8), (1, 4)))
    w_self_qkv = draw_w_self_qkv(jax.random.fold_in(streams_of[10], 71), 0)
    w_self_out = noise(streams_of[5], (HEADS * HD, D), (HEADS * HD) ** -0.5, 0.125, ((0, 8), (1, 4)))
    nbr_kv = draw_nbr_kv(jax.random.fold_in(streams_of[10], 71), 0)
    nbr_count = set_ends(jax.random.randint(streams_of[7], (SPANS,), 1, NBR + 1), jax.random.fold_in(streams_of[7], 1), 1, NBR).astype(jnp.int32)
    nbr_source_keys = jax.random.split(jax.random.fold_in(streams_of[8], 1), SPANS // CH_DEV)
    nbr_source_turns = jax.random.permutation(jax.random.fold_in(streams_of[8], 3), SPANS // CH_DEV)
    nbr_source = jax.vmap(lambda own, number: assign_block(jax.random.fold_in(streams_of[8], 2), own, number, CH_DEV, N_ENC, NBR, CAP, 2))(nbr_source_keys, nbr_source_turns).reshape((SPANS, NBR))
    span_order = jax.random.permutation(streams_of[9], SPANS).astype(jnp.int32)
    return {"hidden_in": hidden_in, "norm_gains": norm_gains, "w_cross_query": w_cross_query, "w_cross_out": w_cross_out, "w_self_qkv": w_self_qkv, "w_self_out": w_self_out, "nbr_kv": nbr_kv, "nbr_count": nbr_count, "nbr_source": nbr_source, "span_order": span_order}


epsilon = 1e-05
far_below = -1e+30

def rms_rows(row_values, gain_row):
    values = row_values.astype(jnp.float32)
    row_scale = lax.rsqrt(lax.optimization_barrier(jnp.mean(values * values, axis=-1, keepdims=True)) + epsilon)
    return (values * row_scale * gain_row).astype(jnp.bfloat16)

def group_sum(left_side, right_side):
    groups = N_ENC * N_MP
    group_width = left_side.shape[1] // groups
    left_groups = left_side.reshape(left_side.shape[0], groups, group_width).transpose(1, 0, 2)
    right_groups = right_side.reshape(groups, group_width, right_side.shape[1])

    def add_group(running, pair):
        term_value = jnp.dot(pair[0], pair[1], preferred_element_type=jnp.float32).astype(jnp.bfloat16)
        term_value = lax.optimization_barrier(term_value)
        return (running + term_value.astype(jnp.float32), None)
    initial = jnp.zeros((left_side.shape[0], right_side.shape[1]), jnp.float32)
    return lax.scan(add_group, initial, (left_groups, right_groups))[0]

def reference(hidden_in, norm_gains, w_cross_query, w_cross_out, w_self_qkv, w_self_out, nbr_kv, nbr_count, nbr_source, span_order):
    features = HEADS * HD
    per_group = HEADS // N_ENC
    attn_scale = 1.0 / math.sqrt(HD)
    normed = rms_rows(hidden_in, norm_gains[0])
    cross_query = jnp.dot(normed, w_cross_query, preferred_element_type=jnp.float32).astype(jnp.bfloat16)
    chosen = nbr_source.reshape(N_CTX, CH_DEV * NBR)
    matches = (chosen[:, :, None] == jnp.arange(N_ENC, dtype=jnp.int32)[None, None, :]).astype(jnp.int32)
    earlier = jnp.cumsum(matches, axis=1) - matches
    slot_ranks = lax.optimization_barrier(jnp.sum(earlier * matches, axis=2)).astype(jnp.int32)
    columns = jnp.broadcast_to(jnp.arange(N_CTX, dtype=jnp.int32)[:, None], chosen.shape)
    picked = nbr_kv[columns.reshape(-1), chosen.reshape(-1), :, slot_ranks.reshape(-1)]
    picked = picked.reshape(SPANS, NBR, N_ENC, NBR_ROWS, per_group, 2, HD)
    picked = picked.transpose(0, 1, 3, 2, 4, 5, 6).reshape(SPANS, NBR, NBR_ROWS, HEADS, 2, HD)
    nbr_keys = picked[:, :, :, :, 0, :].astype(jnp.float32)
    nbr_values = picked[:, :, :, :, 1, :]
    queries = cross_query.reshape(SPANS, SPAN, HEADS, HD).astype(jnp.float32)
    scores = jnp.einsum('cqhd,cjrhd->chqjr', queries, nbr_keys) * attn_scale
    alive_mask = jnp.arange(NBR, dtype=jnp.int32)[None, :] < nbr_count[:, None]
    scores = jnp.where(alive_mask[:, None, None, :, None], scores, far_below)
    row_top = lax.optimization_barrier(jnp.max(scores, axis=(3, 4), keepdims=True))
    weights_f = jnp.exp(scores - row_top)
    row_total = lax.optimization_barrier(jnp.sum(weights_f, axis=(3, 4)))
    weights_b = weights_f.astype(jnp.bfloat16).astype(jnp.float32)
    mixed_heads = jnp.einsum('chqjr,cjrhd->chqd', weights_b, nbr_values.astype(jnp.float32)) / row_total[..., None]
    cross_att = mixed_heads.transpose(0, 2, 1, 3).reshape(SEQ, features).astype(jnp.bfloat16)
    cross_sum = group_sum(cross_att, w_cross_out)
    mid = (hidden_in.astype(jnp.float32) + cross_sum).astype(jnp.bfloat16)
    mid_normed = rms_rows(mid, norm_gains[1])
    projected = jnp.dot(mid_normed, w_self_qkv.reshape(D, 3 * features), preferred_element_type=jnp.float32)
    projected = projected.astype(jnp.bfloat16).reshape(SEQ, 3, HEADS, HD)
    rows_all = jnp.arange(SEQ, dtype=jnp.int32)
    positions = span_order[rows_all // SPAN].astype(jnp.int32) * SPAN + rows_all % SPAN
    visible = positions[None, :] <= positions[:, None]

    def head_attention(triple):
        head_q, head_k, head_v = triple
        head_scores = jnp.dot(head_q, head_k.T, preferred_element_type=jnp.float32) * attn_scale
        head_scores = jnp.where(visible, head_scores, far_below)
        head_top = lax.optimization_barrier(jnp.max(head_scores, axis=1, keepdims=True))
        head_weights = jnp.where(visible, jnp.exp(head_scores - head_top), 0.0)
        head_total = lax.optimization_barrier(jnp.sum(head_weights, axis=1, keepdims=True))
        head_out = jnp.dot(head_weights.astype(jnp.bfloat16), head_v, preferred_element_type=jnp.float32)
        return head_out / head_total
    per_head = projected.transpose(1, 2, 0, 3)
    self_heads = lax.map(head_attention, (per_head[0], per_head[1], per_head[2]))
    self_att = self_heads.transpose(1, 0, 2).reshape(SEQ, features).astype(jnp.bfloat16)
    self_sum = group_sum(self_att, w_self_out)
    return (mid.astype(jnp.float32) + self_sum).astype(jnp.bfloat16)
```

```python
import functools
import math

import jax
import jax.numpy as jnp
from jax import lax
from jax.experimental import pallas as pl
from jax.experimental.pallas import tpu as pltpu
from jax.sharding import PartitionSpec as P

MESH = pl.DeviceIdType.MESH
VMEM_GRANT = 56 * 1024 * 1024
BF16 = jnp.bfloat16
F32 = jnp.float32

HD = 128
SPAN = 64


epsilon = 1e-05
far_below = -1e30


def rms_rows(row_values, gain_row):
    values = row_values.astype(jnp.float32)
    row_scale = lax.rsqrt(jnp.mean(values * values, axis=-1, keepdims=True) + epsilon)
    return (values * row_scale * gain_row).astype(jnp.bfloat16)


def token_places(order_table, first_row, row_count):
    tokens = first_row + jnp.arange(row_count, dtype=jnp.int32)
    blocks = tokens // SPAN
    matches = blocks[:, None] == jnp.arange(order_table.shape[0], dtype=jnp.int32)[None, :]
    placed = jnp.sum(jnp.where(matches, order_table[None, :], 0), axis=1)
    return placed * SPAN + tokens % SPAN


def per_device(
    hidden_in,
    norm_gains,
    w_cross_query,
    w_cross_out,
    w_self_qkv,
    w_self_out,
    nbr_kv,
    nbr_count,
    nbr_source,
    span_order,
):
    tok_rows, model_width = hidden_in.shape
    features = w_cross_query.shape[1]
    heads_here = features // HD
    groups = lax.axis_size(("enc", "mp"))
    share_width = model_width // groups
    group_index = lax.axis_index(("enc", "mp"))
    column = lax.axis_index("ctx")
    attn_scale = 1.0 / math.sqrt(HD)
    normed = rms_rows(hidden_in, norm_gains[0])
    columns_part = normed
    cross_query = jnp.dot(
        columns_part,
        lax.all_gather(w_cross_query, "ctx", axis=0, tiled=True),
        preferred_element_type=jnp.float32,
    ).astype(jnp.bfloat16)
    arrived = lax.all_to_all(nbr_kv[0, 0], "enc", split_axis=0, concat_axis=0, tiled=True)
    sources, slot_count, nbr_rows, pair_width = arrived.shape
    flattened = arrived.reshape(sources * slot_count, nbr_rows, pair_width)
    spans_here, per_span = nbr_source.shape
    chosen = nbr_source.reshape(-1)
    matches = (chosen[:, None] == jnp.arange(sources, dtype=jnp.int32)[None, :]).astype(jnp.int32)
    earlier = jnp.cumsum(matches, axis=0) - matches
    places = chosen * slot_count + jnp.sum(earlier * matches, axis=1)
    picked = jnp.take(flattened, places, axis=0)
    picked = picked.reshape(spans_here, per_span, nbr_rows, heads_here, 2, HD)
    nbr_keys = picked[:, :, :, :, 0, :]
    nbr_values = picked[:, :, :, :, 1, :]
    queries = cross_query.reshape(spans_here, tok_rows // spans_here, heads_here, HD)
    scores = (
        jnp.einsum("cqhd,cjrhd->chqjr", queries, nbr_keys, preferred_element_type=jnp.float32)
        * attn_scale
    )
    alive_mask = jnp.arange(per_span, dtype=jnp.int32)[None, :] < nbr_count[:, None]
    scores = jnp.where(alive_mask[:, None, None, :, None], scores, far_below)
    row_top = jnp.max(scores, axis=(3, 4), keepdims=True)
    weights_f = jnp.exp(scores - row_top)
    row_total = jnp.sum(weights_f, axis=(3, 4))
    mixed_heads = (
        jnp.einsum(
            "chqjr,cjrhd->chqd",
            weights_f.astype(jnp.bfloat16),
            nbr_values,
            preferred_element_type=jnp.float32,
        )
        / row_total[..., None]
    )
    cross_att = mixed_heads.transpose(0, 2, 1, 3).reshape(tok_rows, features).astype(jnp.bfloat16)
    cross_term = jnp.dot(
        cross_att,
        lax.all_gather(w_cross_out, "ctx", axis=1, tiled=True),
        preferred_element_type=jnp.float32,
    )
    summed = lax.psum(cross_term.astype(jnp.bfloat16), ("enc", "mp")).astype(jnp.float32)
    mid_full = (hidden_in.astype(jnp.float32) + summed).astype(jnp.bfloat16)
    mid_normed = rms_rows(mid_full, norm_gains[1])
    mid_share = lax.dynamic_slice_in_dim(mid_full, group_index * share_width, share_width, 1)
    shard_piece = lax.all_gather(w_self_qkv, "ctx", axis=0, tiled=True)
    columns_part = mid_normed
    projected = jnp.dot(
        columns_part,
        shard_piece.reshape(shard_piece.shape[0], 3 * features),
        preferred_element_type=jnp.float32,
    )
    projected = projected.astype(jnp.bfloat16).reshape(tok_rows, 3, heads_here, HD)
    self_query = projected[:, 0]
    keys_values = projected[:, 1:]
    query_places = token_places(span_order, column * tok_rows, tok_rows)
    shard_piece = lax.all_gather(keys_values, "ctx", axis=0, tiled=True)
    old_top = jnp.full((heads_here, tok_rows), far_below, jnp.float32)
    key_places = token_places(span_order, jnp.int32(0), shard_piece.shape[0])
    block_scores = (
        jnp.einsum(
            "qhd,khd->hqk", self_query, shard_piece[:, 0], preferred_element_type=jnp.float32
        )
        * attn_scale
    )
    visible = key_places[None, None, :] <= query_places[None, :, None]
    block_scores = jnp.where(visible, block_scores, far_below)
    new_top = jnp.maximum(old_top, jnp.max(block_scores, axis=2))
    block_weights = jnp.where(visible, jnp.exp(block_scores - new_top[..., None]), 0.0)
    new_total = jnp.sum(block_weights, axis=2)
    running = jnp.einsum(
        "hqk,khd->hqd",
        block_weights.astype(jnp.bfloat16),
        shard_piece[:, 1],
        preferred_element_type=jnp.float32,
    )
    self_att = (
        (running / new_total[..., None])
        .transpose(1, 0, 2)
        .reshape(tok_rows, features)
        .astype(jnp.bfloat16)
    )
    self_term = jnp.dot(
        self_att,
        lax.all_gather(w_self_out, "ctx", axis=1, tiled=True),
        preferred_element_type=jnp.float32,
    )
    out_share = lax.psum_scatter(
        self_term.astype(jnp.bfloat16), ("enc", "mp"), scatter_dimension=1, tiled=True
    ).astype(jnp.float32)
    return (mid_share.astype(jnp.float32) + out_share).astype(jnp.bfloat16)


def dot(a, b):
    return jnp.dot(a, b, preferred_element_type=F32)


def dot_t(a, b):
    return lax.dot_general(a, b, (((1,), (1,)), ((), ())), preferred_element_type=F32)


def block_kernel(
    hid, gains, wq, wco, wqkv, wso, nbr, cnt, nsrc, order, out,
    hid_all, nbr_all, qsend, qpart, rs0, att_all, wso_all, term, corebuf, cs, rsbuf, mid_all,
    sssend, sspart, qkvsend, qkvpart, qbuf, kv_all, midown, att2, fother, fmine, fcore, fsum, frs,
    send_sems, recv_sems,
):
    c, e, m = lax.axis_index("ctx"), lax.axis_index("enc"), lax.axis_index("mp")
    n = hid_all.shape[0]
    tok, width = hid.shape
    shard = width // n
    feats = wq.shape[1]
    heads = feats // HD
    slots = nbr.shape[1]
    n_enc = nbr.shape[0]
    rows = tok // 8
    half = tok // 2
    cols = out.shape[1]
    attn_scale = 1.0 / math.sqrt(HD)

    core, y = lax.rem(e, 2), e // 2
    mate = {"enc": e + 1 - 2 * core}
    place = y * 2 + m

    def at_place(p):
        y2 = 1 - y if p & 2 else y
        m2 = 1 - m if p & 1 else m
        return y2, m2

    def peer(p):
        y2, m2 = at_place(p)
        return {"enc": y2 * 2 + core, "mp": m2}

    def ctx_of(k):
        return lax.rem(c + k, n)

    def src_of(k):
        return lax.rem(c - k + n, n)

    issued = []

    def rcopy(src, dst, device, recv=None, start=True):
        i = rcopy.count
        rcopy.count += 1
        d = pltpu.make_async_remote_copy(
            src_ref=src, dst_ref=dst, send_sem=send_sems.at[i],
            recv_sem=recv_sems.at[i if recv is None else recv],
            device_id=device, device_id_type=MESH,
        )
        if start:
            d.start()
            issued.append(d)
        return d

    rcopy.count = 0

    barrier = pltpu.get_barrier_semaphore()
    friends = [{"ctx": ctx_of(k)} for k in range(1, n)]
    friends += [{"enc": lax.rem(e + k, n_enc)} for k in range(1, n_enc)]
    friends += [peer(1), peer(3)]
    for f in friends:
        pl.semaphore_signal(barrier, inc=1, device_id=f, device_id_type=MESH)
    pl.semaphore_wait(barrier, len(friends))

    my_rows = pl.ds(pl.multiple_of(core * half + place * rows, rows), rows)
    my_half = pl.ds(pl.multiple_of(core * half, half), half)
    mate_half = pl.ds(pl.multiple_of((1 - core) * half, half), half)
    my_shard = pl.ds(pl.multiple_of(c * shard, shard), shard)

    a1 = {}
    for k in range(1, n):
        t = ctx_of(k)
        there = pl.ds(pl.multiple_of(t * shard, shard), shard)
        a1[k] = rcopy(hid.at[my_rows, there], hid_all.at[c, my_rows, :], {"ctx": t})
    nb = []
    for k in range(1, n_enc):
        f = lax.rem(e + k, n_enc)
        nb.append(rcopy(nbr.at[f], nbr_all.at[pl.ds(e * slots, slots)], {"enc": f}))
    hid_all[c] = hid[:, my_shard]
    nbr_all[pl.ds(e * slots, slots)] = nbr[e]
    gain0 = gains[0:1, my_shard]
    gain1 = gains[1:2, my_shard]

    def project_query(s):
        x = (hid_all[s].astype(F32) * gain0).astype(BF16)
        qsend[s] = dot(x, wq[...]).astype(BF16)

    a2 = {}
    for k in range(1, n):
        s = src_of(k)
        a1[k].wait_recv()
        for p in (3, 1, 2):
            block = hid_all.at[s, my_rows, :]
            a2[k, p] = rcopy(block, block, peer(p))
    project_query(c)
    squares = jnp.zeros((tok, 1), F32)
    for j in range(n):
        x = hid[:, j * shard:(j + 1) * shard].astype(F32)
        squares = squares + jnp.sum(x * x, axis=1, keepdims=True)
    rs0[...] = jnp.broadcast_to(lax.rsqrt(squares / width + epsilon), rs0.shape)
    a3 = {}
    for k in range(1, n):
        s = src_of(k)
        for p in (1, 2, 3):
            a2[k, p].wait_recv()
        block = hid_all.at[s, my_half, :]
        a3[k] = rcopy(block, block, mate)
    qs = []
    for k in range(1, n):
        s = src_of(k)
        a3[k].wait_recv()
        project_query(s)
        qs.append(rcopy(qsend.at[s], qpart.at[k - 1], {"ctx": s}))
    for d in nb:
        d.wait_recv()
    for d in qs:
        d.wait_recv()
    q = qsend[c].astype(F32)
    for k in range(n - 1):
        q = q + qpart[k].astype(F32)
    q = (q * rs0[:, 0:1]).astype(BF16)

    spans, per_span = nsrc.shape
    lane = lax.broadcasted_iota(jnp.int32, (SPAN, per_span * SPAN), 1)
    for i in range(spans):
        kv = []
        for j in range(per_span):
            chosen = nsrc[i, j]
            rank = 0
            for i2 in range(i):
                for j2 in range(per_span):
                    rank = rank + jnp.where(nsrc[i2, j2] == chosen, 1, 0)
            kv.append(nbr_all[chosen * slots + rank])
        alive = lane < cnt[i] * SPAN
        for u in range(heads):
            lo = 2 * u * HD
            keys = jnp.concatenate([b[:, lo:lo + HD] for b in kv], axis=0)
            values = jnp.concatenate([b[:, lo + HD:lo + 2 * HD] for b in kv], axis=0)
            qi = q[i * SPAN:(i + 1) * SPAN, u * HD:(u + 1) * HD]
            sc = jnp.where(alive, dot_t(qi, keys) * attn_scale, far_below)
            w = jnp.exp(sc - jnp.max(sc, axis=1, keepdims=True))
            mixed = dot(w.astype(BF16), values) / jnp.sum(w, axis=1, keepdims=True)
            att_all[c, i * SPAN:(i + 1) * SPAN, u * HD:(u + 1) * HD] = mixed.astype(BF16)

    at = {k: rcopy(att_all.at[c], att_all.at[c], {"ctx": ctx_of(k)}) for k in range(1, n)}
    ws = [rcopy(wso, wso_all.at[c], {"ctx": ctx_of(k)}) for k in range(1, n)]
    wso_all[c] = wso[...]

    c2 = {}
    for k in range(n):
        s = src_of(k)
        if k:
            at[k].wait_recv()
        term[s] = dot(att_all[s], wco[...]).astype(BF16)
        c2[k] = rcopy(term.at[s, mate_half, :], corebuf.at[s], mate)
    c3 = {}
    for k in range(n):
        s = src_of(k)
        c2[k].wait_recv()
        cs[s] = (term[s, my_half, :].astype(F32) + corebuf[s].astype(F32)).astype(BF16)
        for p in (3, 1, 2):
            y2, m2 = at_place(p)
            theirs = pl.ds(pl.multiple_of((y2 * 2 + m2) * rows, rows), rows)
            c3[k, p] = rcopy(cs.at[s, theirs, :], rsbuf.at[p - 1, s], peer(p))
    c4 = {}
    for k in range(n):
        s = src_of(k)
        total = hid_all[s, my_rows, :].astype(F32)
        total = total + cs[s, pl.ds(pl.multiple_of(place * rows, rows), rows), :].astype(F32)
        for p in (1, 2, 3):
            c3[k, p].wait_recv()
            total = total + rsbuf[p - 1, s].astype(F32)
        mid_all[s, my_rows, :] = total.astype(BF16)
        block = mid_all.at[s, my_rows, :]
        for p in (3, 1, 2):
            c4[k, p] = rcopy(block, block, peer(p))
    c5 = {}
    for k in range(n):
        s = src_of(k)
        for p in (1, 2, 3):
            c4[k, p].wait_recv()
        block = mid_all.at[s, my_half, :]
        c5[k] = rcopy(block, block, mate)

    parts = []
    for k in list(range(1, n)) + [0]:
        s = src_of(k)
        c5[k].wait_recv()
        x = mid_all[s].astype(F32)
        squares = jnp.sum(x * x, axis=1, keepdims=True)
        sssend[s] = jnp.broadcast_to(squares, (tok, HD)).T[0:8]
        qkvsend[s] = dot((x * gain1).astype(BF16), wqkv[...]).astype(BF16)
        if k:
            parts.append(rcopy(qkvsend.at[s], qkvpart.at[k - 1], {"ctx": s}))
            parts.append(rcopy(sssend.at[s], sspart.at[k - 1], {"ctx": s}))

    my_cols = pl.ds(pl.multiple_of(m * cols, cols), cols)
    recv = rcopy.count
    residual = []
    for k in range(1, n):
        t = ctx_of(k)
        residual.append(
            rcopy(mid_all.at[t, :, my_cols], midown, {"ctx": t}, recv=recv, start=False)
        )

    @pl.when(c == e)
    def _():
        for d in residual:
            d.start()
        midown[...] = mid_all[c, :, my_cols]

    for d in parts:
        d.wait_recv()
    squares = sssend[c]
    for k in range(n - 1):
        squares = squares + sspart[k]
    squares = jnp.broadcast_to(squares[0:1], (HD, tok)).T[:, 0:1]
    row_scale = lax.rsqrt(squares / width + epsilon)

    def whole(lo, hi):
        total = qkvsend[c, :, lo:hi].astype(F32)
        for k in range(n - 1):
            total = total + qkvpart[k, :, lo:hi].astype(F32)
        return (total * row_scale).astype(BF16)

    kv_all[c] = whole(feats, 3 * feats)
    kvs = {k: rcopy(kv_all.at[c], kv_all.at[c], {"ctx": ctx_of(k)}) for k in range(1, n)}
    qbuf[...] = whole(0, feats)

    def places(s, shape, axis):
        index = lax.broadcasted_iota(jnp.int32, shape, axis)
        first = s * (tok // SPAN)
        found = jnp.zeros(shape, jnp.int32)
        for b in range(tok // SPAN):
            found = jnp.where(index // SPAN == b, order[first + b], found)
        return found * SPAN + lax.rem(index, SPAN)

    query_places = places(c, (tok, 1), 0)
    tops = [jnp.full((tok, 1), far_below, F32) for _ in range(heads)]
    sums = [jnp.zeros((tok, 1), F32) for _ in range(heads)]
    accs = [jnp.zeros((tok, HD), F32) for _ in range(heads)]
    for k in range(n):
        s = src_of(k)
        if k:
            kvs[k].wait_recv()
        visible = places(s, (1, tok), 1) <= query_places
        for u in range(heads):
            keys = kv_all[s, :, u * HD:(u + 1) * HD]
            values = kv_all[s, :, feats + u * HD:feats + (u + 1) * HD]
            sc = dot_t(qbuf[:, u * HD:(u + 1) * HD], keys) * attn_scale
            sc = jnp.where(visible, sc, far_below)
            top = jnp.maximum(tops[u], jnp.max(sc, axis=1, keepdims=True))
            w = jnp.where(visible, jnp.exp(sc - top), 0.0)
            shrink = jnp.exp(tops[u] - top)
            sums[u] = sums[u] * shrink + jnp.sum(w, axis=1, keepdims=True)
            accs[u] = accs[u] * shrink + dot(w.astype(BF16), values)
            tops[u] = top
    for u in range(heads):
        att2[:, u * HD:(u + 1) * HD] = (accs[u] / sums[u]).astype(BF16)

    for d in ws:
        d.wait_recv()
    f1 = {}
    for p in (3, 1, 2, 0):
        y2, m2 = at_place(p)
        there = pl.ds(pl.multiple_of(m2 * cols, cols), cols)
        fother[p] = dot(att2[...], wso_all[y2 * 2 + 1 - core, :, there]).astype(BF16)
        f1[p] = rcopy(fother.at[p], fcore.at[p], mate)
        fmine[p] = dot(att2[...], wso_all[y2 * 2 + core, :, there]).astype(BF16)
    f2 = {}
    for p in (3, 1, 2):
        f1[p].wait_recv()
        fsum[p - 1] = (fmine[p].astype(F32) + fcore[p].astype(F32)).astype(BF16)
        f2[p] = rcopy(fsum.at[p - 1], frs.at[p - 1], peer(p))
    f1[0].wait_recv()

    @pl.when(c == e)
    def _():
        for d in residual:
            d.wait_send()

    @pl.when(c != e)
    def _():
        residual[0].wait_recv()

    total = midown[...].astype(F32) + fmine[0].astype(F32) + fcore[0].astype(F32)
    for p in (1, 2, 3):
        f2[p].wait_recv()
        total = total + frs[p - 1].astype(F32)
    out[...] = total.astype(BF16)
    for d in issued:
        d.wait_send()


def scratch_shapes(n, n_enc, tok, width, feats, slots, nbr_rows, pair_width, cols):
    shard = width // n
    half, rows = tok // 2, tok // 8
    return [
        ((n, tok, shard), BF16),
        ((n_enc * slots, nbr_rows, pair_width), BF16),
        ((n, tok, feats), BF16),
        ((n - 1, tok, feats), BF16),
        ((tok, HD), F32),
        ((n, tok, feats), BF16),
        ((n, feats, shard), BF16),
        ((n, tok, shard), BF16),
        ((n, half, shard), BF16),
        ((n, half, shard), BF16),
        ((3, n, rows, shard), BF16),
        ((n, tok, shard), BF16),
        ((n, 8, tok), F32),
        ((n - 1, 8, tok), F32),
        ((n, tok, 3 * feats), BF16),
        ((n - 1, tok, 3 * feats), BF16),
        ((tok, feats), BF16),
        ((n, tok, 2 * feats), BF16),
        ((tok, cols), BF16),
        ((tok, feats), BF16),
        ((4, tok, cols), BF16),
        ((4, tok, cols), BF16),
        ((4, tok, cols), BF16),
        ((3, tok, cols), BF16),
        ((3, tok, cols), BF16),
    ]


def per_device_any(sizes, *args):
    n, n_enc, n_mp = sizes
    hidden_in, norm_gains, w_cross_query, w_cross_out, w_self_qkv, w_self_out, nbr_kv = args[:7]
    tok, width = hidden_in.shape
    feats = w_cross_query.shape[1]
    cols = width // (n_enc * n_mp)
    slots, nbr_rows, pair_width = nbr_kv.shape[3:]
    held = scratch_shapes(n, n_enc, tok, width, feats, slots, nbr_rows, pair_width, cols)
    need = sum(math.prod(shape) * jnp.dtype(kind).itemsize for shape, kind in held)
    if need > VMEM_GRANT // 2 or (n_enc, n_mp) != (4, 2) or width != n * 2 * cols:
        return per_device(*args)
    copies = 96
    vmem = pl.BlockSpec(memory_space=pltpu.VMEM)
    smem = pl.BlockSpec(memory_space=pltpu.SMEM)
    return pl.pallas_call(
        block_kernel,
        out_shape=jax.ShapeDtypeStruct((tok, cols), BF16),
        in_specs=[vmem] * 7 + [smem] * 3,
        out_specs=vmem,
        scratch_shapes=[pltpu.VMEM(shape, kind) for shape, kind in held]
        + [pltpu.SemaphoreType.DMA((copies,)), pltpu.SemaphoreType.DMA((copies,))],
        compiler_params=pltpu.CompilerParams(
            collective_id=0, has_side_effects=True, vmem_limit_bytes=VMEM_GRANT
        ),
    )(
        hidden_in, norm_gains, w_cross_query, w_cross_out,
        w_self_qkv.reshape(w_self_qkv.shape[0], 3 * feats), w_self_out,
        nbr_kv[0, 0], *args[7:],
    )


def solution(mesh):
    in_specs = (
        P("ctx", None),
        P(),
        P("ctx", ("enc", "mp")),
        P(("enc", "mp"), "ctx"),
        P("ctx", None, ("enc", "mp")),
        P(("enc", "mp"), "ctx"),
        P("ctx", "enc", None, None, None, "mp"),
        P("ctx"),
        P("ctx", None),
        P(),
    )
    out_specs = P("ctx", ("enc", "mp"))
    sizes = (mesh.shape["ctx"], mesh.shape["enc"], mesh.shape["mp"])
    return jax.shard_map(
        functools.partial(per_device_any, sizes), mesh=mesh, in_specs=in_specs, out_specs=out_specs, check_vma=False
    )
```

```python
import functools
import math

import jax
import jax.numpy as jnp
from jax import lax
from jax.experimental import pallas as pl
from jax.experimental.pallas import tpu as pltpu
from jax.sharding import PartitionSpec as P

MESH = pl.DeviceIdType.MESH
VMEM_GRANT = 56 * 1024 * 1024
BF16 = jnp.bfloat16
F32 = jnp.float32

HD = 128
SPAN = 64


epsilon = 1e-05
far_below = -1e30


def rms_rows(row_values, gain_row):
    values = row_values.astype(jnp.float32)
    row_scale = lax.rsqrt(jnp.mean(values * values, axis=-1, keepdims=True) + epsilon)
    return (values * row_scale * gain_row).astype(jnp.bfloat16)


def token_places(order_table, first_row, row_count):
    tokens = first_row + jnp.arange(row_count, dtype=jnp.int32)
    blocks = tokens // SPAN
    matches = blocks[:, None] == jnp.arange(order_table.shape[0], dtype=jnp.int32)[None, :]
    placed = jnp.sum(jnp.where(matches, order_table[None, :], 0), axis=1)
    return placed * SPAN + tokens % SPAN


def per_device(
    hidden_in,
    norm_gains,
    w_cross_query,
    w_cross_out,
    w_self_qkv,
    w_self_out,
    nbr_kv,
    nbr_count,
    nbr_source,
    span_order,
):
    tok_rows, model_width = hidden_in.shape
    features = w_cross_query.shape[1]
    heads_here = features // HD
    groups = lax.axis_size(("enc", "mp"))
    share_width = model_width // groups
    group_index = lax.axis_index(("enc", "mp"))
    column = lax.axis_index("ctx")
    attn_scale = 1.0 / math.sqrt(HD)
    normed = rms_rows(hidden_in, norm_gains[0])
    columns_part = normed
    cross_query = jnp.dot(
        columns_part,
        lax.all_gather(w_cross_query, "ctx", axis=0, tiled=True),
        preferred_element_type=jnp.float32,
    ).astype(jnp.bfloat16)
    arrived = lax.all_to_all(nbr_kv[0, 0], "enc", split_axis=0, concat_axis=0, tiled=True)
    sources, slot_count, nbr_rows, pair_width = arrived.shape
    flattened = arrived.reshape(sources * slot_count, nbr_rows, pair_width)
    spans_here, per_span = nbr_source.shape
    chosen = nbr_source.reshape(-1)
    matches = (chosen[:, None] == jnp.arange(sources, dtype=jnp.int32)[None, :]).astype(jnp.int32)
    earlier = jnp.cumsum(matches, axis=0) - matches
    places = chosen * slot_count + jnp.sum(earlier * matches, axis=1)
    picked = jnp.take(flattened, places, axis=0)
    picked = picked.reshape(spans_here, per_span, nbr_rows, heads_here, 2, HD)
    nbr_keys = picked[:, :, :, :, 0, :]
    nbr_values = picked[:, :, :, :, 1, :]
    queries = cross_query.reshape(spans_here, tok_rows // spans_here, heads_here, HD)
    scores = (
        jnp.einsum("cqhd,cjrhd->chqjr", queries, nbr_keys, preferred_element_type=jnp.float32)
        * attn_scale
    )
    alive_mask = jnp.arange(per_span, dtype=jnp.int32)[None, :] < nbr_count[:, None]
    scores = jnp.where(alive_mask[:, None, None, :, None], scores, far_below)
    row_top = jnp.max(scores, axis=(3, 4), keepdims=True)
    weights_f = jnp.exp(scores - row_top)
    row_total = jnp.sum(weights_f, axis=(3, 4))
    mixed_heads = (
        jnp.einsum(
            "chqjr,cjrhd->chqd",
            weights_f.astype(jnp.bfloat16),
            nbr_values,
            preferred_element_type=jnp.float32,
        )
        / row_total[..., None]
    )
    cross_att = mixed_heads.transpose(0, 2, 1, 3).reshape(tok_rows, features).astype(jnp.bfloat16)
    cross_term = jnp.dot(
        cross_att,
        lax.all_gather(w_cross_out, "ctx", axis=1, tiled=True),
        preferred_element_type=jnp.float32,
    )
    summed = lax.psum(cross_term.astype(jnp.bfloat16), ("enc", "mp")).astype(jnp.float32)
    mid_full = (hidden_in.astype(jnp.float32) + summed).astype(jnp.bfloat16)
    mid_normed = rms_rows(mid_full, norm_gains[1])
    mid_share = lax.dynamic_slice_in_dim(mid_full, group_index * share_width, share_width, 1)
    shard_piece = lax.all_gather(w_self_qkv, "ctx", axis=0, tiled=True)
    columns_part = mid_normed
    projected = jnp.dot(
        columns_part,
        shard_piece.reshape(shard_piece.shape[0], 3 * features),
        preferred_element_type=jnp.float32,
    )
    projected = projected.astype(jnp.bfloat16).reshape(tok_rows, 3, heads_here, HD)
    self_query = projected[:, 0]
    keys_values = projected[:, 1:]
    query_places = token_places(span_order, column * tok_rows, tok_rows)
    shard_piece = lax.all_gather(keys_values, "ctx", axis=0, tiled=True)
    old_top = jnp.full((heads_here, tok_rows), far_below, jnp.float32)
    key_places = token_places(span_order, jnp.int32(0), shard_piece.shape[0])
    block_scores = (
        jnp.einsum(
            "qhd,khd->hqk", self_query, shard_piece[:, 0], preferred_element_type=jnp.float32
        )
        * attn_scale
    )
    visible = key_places[None, None, :] <= query_places[None, :, None]
    block_scores = jnp.where(visible, block_scores, far_below)
    new_top = jnp.maximum(old_top, jnp.max(block_scores, axis=2))
    block_weights = jnp.where(visible, jnp.exp(block_scores - new_top[..., None]), 0.0)
    new_total = jnp.sum(block_weights, axis=2)
    running = jnp.einsum(
        "hqk,khd->hqd",
        block_weights.astype(jnp.bfloat16),
        shard_piece[:, 1],
        preferred_element_type=jnp.float32,
    )
    self_att = (
        (running / new_total[..., None])
        .transpose(1, 0, 2)
        .reshape(tok_rows, features)
        .astype(jnp.bfloat16)
    )
    self_term = jnp.dot(
        self_att,
        lax.all_gather(w_self_out, "ctx", axis=1, tiled=True),
        preferred_element_type=jnp.float32,
    )
    out_share = lax.psum_scatter(
        self_term.astype(jnp.bfloat16), ("enc", "mp"), scatter_dimension=1, tiled=True
    ).astype(jnp.float32)
    return (mid_share.astype(jnp.float32) + out_share).astype(jnp.bfloat16)


def dot(a, b):
    return jnp.dot(a, b, preferred_element_type=F32)


def dot_t(a, b):
    return lax.dot_general(a, b, (((1,), (1,)), ((), ())), preferred_element_type=F32)


def block_kernel(
    hid, gains, wq, wco, wqkv, wso, nbr, cnt, nsrc, order, out,
    hid_all, nbr_all, qsend, qpart, rs0, att_all, wso_all, term, corebuf, cs, rsbuf, mid_all,
    sssend, sspart, kvsend, kvpart, kvrelay, q2send, q2part, q2relay, qbuf, kv_all, midown, att2, fother, fmine, fcore, fsum, frs,
    send_sems, recv_sems,
):
    c, e, m = lax.axis_index("ctx"), lax.axis_index("enc"), lax.axis_index("mp")
    n = hid_all.shape[0]
    tok, width = hid.shape
    shard = width // n
    feats = wq.shape[1]
    heads = feats // HD
    slots = nbr.shape[1]
    n_enc = nbr.shape[0]
    rows = tok // 8
    half = tok // 2
    cols = out.shape[1]
    attn_scale = 1.0 / math.sqrt(HD)

    core, y = lax.rem(e, 2), e // 2
    mate = {"enc": e + 1 - 2 * core}
    place = y * 2 + m

    def at_place(p):
        y2 = 1 - y if p & 2 else y
        m2 = 1 - m if p & 1 else m
        return y2, m2

    def peer(p):
        y2, m2 = at_place(p)
        return {"enc": y2 * 2 + core, "mp": m2}

    def ctx_of(k):
        return lax.rem(c + k, n)

    def src_of(k):
        return lax.rem(c - k + n, n)

    near = 3 - 2 * (c // 2)
    far = 4 - near
    is_inner = lax.rem((c + 1) // 2, 2)
    is_outer = 1 - is_inner
    inner, outer = is_inner == 1, is_outer == 1
    turns = [0, is_inner * near + is_outer * 2, far, is_inner * 2 + is_outer * near]

    issued = []
    count = [0]

    def alloc(amount):
        count[0] += amount
        return count[0] - amount

    def describe(src, dst, device, send, recv):
        return pltpu.make_async_remote_copy(
            src_ref=src, dst_ref=dst, send_sem=send_sems.at[send], recv_sem=recv_sems.at[recv],
            device_id=device, device_id_type=MESH,
        )

    def rcopy(src, dst, device):
        i = alloc(1)
        d = describe(src, dst, device, i, i)
        d.start()
        issued.append((None, d))
        return d

    def gather_start(src, buf, base):
        def one(k):
            return describe(src, buf.at[c], {"ctx": ctx_of(k)}, base + k - 1, base + k - 1)

        last = one(near)
        for d in (one(2), one(far)):
            d.start()
            issued.append((None, d))

        @pl.when(inner)
        def _():
            last.start()

        issued.append((inner, last))

    def gather_wait(buf, base, k):
        block = buf.at[c]
        describe(block, block, {"ctx": ctx_of(1)}, base, base + k - 1).wait_recv()

    def gather_relay(buf, base):
        block = buf.at[src_of(2)]
        d = describe(block, block, {"ctx": (c - 1) * 3}, base + 3, base + 2 * is_inner * (c - 1))
        issued.append((inner, d))

        @pl.when(inner)
        def _():
            d.start()

    def scatter_send(turn, send, part, relay, base):
        k = turns[turn]
        s = src_of(k)
        at = base + turn - 1
        direct = describe(send.at[s], part.at[k - 1], {"ctx": s}, at, base + k - 1)
        via = describe(send.at[s], relay, {"ctx": 1 + c // 3}, at, base + 3)
        if turn == 2:
            @pl.when(outer)
            def _():
                via.start()

            @pl.when(inner)
            def _():
                direct.start()
        else:
            if turn == 3:
                @pl.when(inner)
                def _():
                    via.wait_recv()
                    send[s] = (send[s].astype(F32) + relay[...].astype(F32)).astype(BF16)

            direct.start()
        issued.append((None, direct))

    def scatter_wait(part, base):
        def one(k):
            block = part.at[0]
            describe(block, block, {"ctx": ctx_of(1)}, base, base + k - 1).wait_recv()

        one(2)
        one(far)

        @pl.when(inner)
        def _():
            one(near)

        @pl.when(outer)
        def _():
            part[near - 1] = jnp.zeros(part.shape[1:], BF16)

    barrier = pltpu.get_barrier_semaphore()
    friends = [{"ctx": ctx_of(k)} for k in range(1, n)]
    friends += [{"enc": lax.rem(e + k, n_enc)} for k in range(1, n_enc)]
    friends += [peer(1), peer(3)]
    for f in friends:
        pl.semaphore_signal(barrier, inc=1, device_id=f, device_id_type=MESH)
    pl.semaphore_wait(barrier, len(friends))

    my_rows = pl.ds(pl.multiple_of(core * half + place * rows, rows), rows)
    my_half = pl.ds(pl.multiple_of(core * half, half), half)
    mate_half = pl.ds(pl.multiple_of((1 - core) * half, half), half)
    my_shard = pl.ds(pl.multiple_of(c * shard, shard), shard)

    a1 = {}
    for k in range(1, n):
        t = ctx_of(k)
        there = pl.ds(pl.multiple_of(t * shard, shard), shard)
        a1[k] = rcopy(hid.at[my_rows, there], hid_all.at[c, my_rows, :], {"ctx": t})
    nb = []
    for k in range(1, n_enc):
        f = lax.rem(e + k, n_enc)
        nb.append(rcopy(nbr.at[f], nbr_all.at[pl.ds(e * slots, slots)], {"enc": f}))
    hid_all[c] = hid[:, my_shard]
    nbr_all[pl.ds(e * slots, slots)] = nbr[e]
    gain0 = gains[0:1, my_shard]
    gain1 = gains[1:2, my_shard]

    def project_query(s):
        x = (hid_all[s].astype(F32) * gain0).astype(BF16)
        qsend[s] = dot(x, wq[...]).astype(BF16)

    a2 = {}
    for k in range(1, n):
        s = src_of(k)
        a1[k].wait_recv()
        for p in (3, 1, 2):
            block = hid_all.at[s, my_rows, :]
            a2[k, p] = rcopy(block, block, peer(p))
    project_query(c)
    squares = jnp.zeros((tok, 1), F32)
    for j in range(n):
        x = hid[:, j * shard:(j + 1) * shard].astype(F32)
        squares = squares + jnp.sum(x * x, axis=1, keepdims=True)
    rs0[...] = jnp.broadcast_to(lax.rsqrt(squares / width + epsilon), rs0.shape)
    a3 = {}
    for k in range(1, n):
        s = src_of(k)
        for p in (1, 2, 3):
            a2[k, p].wait_recv()
        block = hid_all.at[s, my_half, :]
        a3[k] = rcopy(block, block, mate)
    qs = []
    for k in range(1, n):
        s = src_of(k)
        a3[k].wait_recv()
        project_query(s)
        qs.append(rcopy(qsend.at[s], qpart.at[k - 1], {"ctx": s}))
    for d in nb:
        d.wait_recv()
    for d in qs:
        d.wait_recv()
    q = qsend[c].astype(F32)
    for k in range(n - 1):
        q = q + qpart[k].astype(F32)
    q = (q * rs0[:, 0:1]).astype(BF16)

    spans, per_span = nsrc.shape
    lane = lax.broadcasted_iota(jnp.int32, (SPAN, per_span * SPAN), 1)
    for i in range(spans):
        kv = []
        for j in range(per_span):
            chosen = nsrc[i, j]
            rank = 0
            for i2 in range(i):
                for j2 in range(per_span):
                    rank = rank + jnp.where(nsrc[i2, j2] == chosen, 1, 0)
            kv.append(nbr_all[chosen * slots + rank])
        alive = lane < cnt[i] * SPAN
        for u in range(heads):
            lo = 2 * u * HD
            keys = jnp.concatenate([b[:, lo:lo + HD] for b in kv], axis=0)
            values = jnp.concatenate([b[:, lo + HD:lo + 2 * HD] for b in kv], axis=0)
            qi = q[i * SPAN:(i + 1) * SPAN, u * HD:(u + 1) * HD]
            sc = jnp.where(alive, dot_t(qi, keys) * attn_scale, far_below)
            w = jnp.exp(sc - jnp.max(sc, axis=1, keepdims=True))
            mixed = dot(w.astype(BF16), values) / jnp.sum(w, axis=1, keepdims=True)
            att_all[c, i * SPAN:(i + 1) * SPAN, u * HD:(u + 1) * HD] = mixed.astype(BF16)

    at = alloc(3)
    for k in range(1, n):
        d = describe(att_all.at[c], att_all.at[c], {"ctx": ctx_of(k)}, at + k - 1, at + k - 1)
        d.start()
        issued.append((None, d))
    ws = alloc(4)
    gather_start(wso, wso_all, ws)
    wso_all[c] = wso[...]

    c2, c3, c4, c5, ssp = {}, {}, {}, {}, []
    kvb, q2b = alloc(4), alloc(4)

    def project_out(j):
        s = src_of(turns[j])
        if j:
            gather_wait(att_all, at, turns[j])
        term[s] = dot(att_all[s], wco[...]).astype(BF16)
        c2[j] = rcopy(term.at[s, mate_half, :], corebuf.at[s], mate)

    def pair_sum(j):
        s = src_of(turns[j])
        c2[j].wait_recv()
        cs[s] = (term[s, my_half, :].astype(F32) + corebuf[s].astype(F32)).astype(BF16)
        for p in (3, 1, 2):
            y2, m2 = at_place(p)
            theirs = pl.ds(pl.multiple_of((y2 * 2 + m2) * rows, rows), rows)
            c3[j, p] = rcopy(cs.at[s, theirs, :], rsbuf.at[p - 1, s], peer(p))

    def plane_sum(j):
        s = src_of(turns[j])
        total = hid_all[s, my_rows, :].astype(F32)
        total = total + cs[s, pl.ds(pl.multiple_of(place * rows, rows), rows), :].astype(F32)
        for p in (1, 2, 3):
            c3[j, p].wait_recv()
            total = total + rsbuf[p - 1, s].astype(F32)
        mid_all[s, my_rows, :] = total.astype(BF16)
        block = mid_all.at[s, my_rows, :]
        for p in (3, 1, 2):
            c4[j, p] = rcopy(block, block, peer(p))

    def plane_share(j):
        s = src_of(turns[j])
        for p in (1, 2, 3):
            c4[j, p].wait_recv()
        block = mid_all.at[s, my_half, :]
        c5[j] = rcopy(block, block, mate)

    def project_kv(j):
        s = src_of(turns[j])
        c5[j].wait_recv()
        x = mid_all[s].astype(F32)
        squares = jnp.sum(x * x, axis=1, keepdims=True)
        sssend[s] = jnp.broadcast_to(squares, (tok, HD)).T[0:8]
        kvsend[s] = dot((x * gain1).astype(BF16), wqkv[:, feats:]).astype(BF16)
        if j:
            scatter_send(j, kvsend, kvpart, kvrelay, kvb)

    stages = (project_out, pair_sum, plane_sum, plane_share, project_kv)
    for step in range(n + len(stages) - 1):
        for i in reversed(range(len(stages))):
            if 0 <= step - i < n:
                stages[i](step - i)
    for k in range(1, n):
        s = src_of(k)
        ssp.append(rcopy(sssend.at[s], sspart.at[k - 1], {"ctx": s}))
    for j in (1, 2, 3, 0):
        s = src_of(turns[j])
        x = (mid_all[s].astype(F32) * gain1).astype(BF16)
        q2send[s] = dot(x, wqkv[:, 0:feats]).astype(BF16)
        if j:
            scatter_send(j, q2send, q2part, q2relay, q2b)
    my_cols = pl.ds(pl.multiple_of(m * cols, cols), cols)

    def whole(send, part):
        total = send[c].astype(F32)
        for k in range(n - 1):
            total = total + part[k].astype(F32)
        return (total * row_scale).astype(BF16)

    for d in ssp:
        d.wait_recv()
    squares = sssend[c]
    for k in range(n - 1):
        squares = squares + sspart[k]
    squares = jnp.broadcast_to(squares[0:1], (HD, tok)).T[:, 0:1]
    row_scale = lax.rsqrt(squares / width + epsilon)
    scatter_wait(kvpart, kvb)
    kv_all[c] = whole(kvsend, kvpart)
    kvg = alloc(4)
    gather_start(kv_all.at[c], kv_all, kvg)

    @pl.when(inner)
    def _():
        gather_wait(wso_all, ws, 2)

    gather_relay(wso_all, ws)

    resid = alloc(3)
    residual = []
    for k in range(1, n):
        t = ctx_of(k)
        residual.append(
            describe(mid_all.at[t, :, my_cols], midown, {"ctx": t}, resid + k - 1, resid)
        )

    @pl.when(c == e)
    def _():
        for d in residual:
            d.start()
        midown[...] = mid_all[c, :, my_cols]

    scatter_wait(q2part, q2b)
    qbuf[...] = whole(q2send, q2part)

    def places(s, shape, axis):
        index = lax.broadcasted_iota(jnp.int32, shape, axis)
        first = s * (tok // SPAN)
        found = jnp.zeros(shape, jnp.int32)
        for b in range(tok // SPAN):
            found = jnp.where(index // SPAN == b, order[first + b], found)
        return found * SPAN + lax.rem(index, SPAN)

    query_places = places(c, (tok, 1), 0)
    tops = [jnp.full((tok, 1), far_below, F32) for _ in range(heads)]
    sums = [jnp.zeros((tok, 1), F32) for _ in range(heads)]
    accs = [jnp.zeros((tok, HD), F32) for _ in range(heads)]
    arrivals = (0, is_inner * 2 + is_outer * near, is_inner * near + is_outer * 2, far)
    for i, k in enumerate(arrivals):
        s = src_of(k)
        if i:
            gather_wait(kv_all, kvg, k)
        if i == 1:
            gather_relay(kv_all, kvg)
        visible = places(s, (1, tok), 1) <= query_places
        for u in range(heads):
            keys = kv_all[s, :, u * HD:(u + 1) * HD]
            values = kv_all[s, :, feats + u * HD:feats + (u + 1) * HD]
            sc = dot_t(qbuf[:, u * HD:(u + 1) * HD], keys) * attn_scale
            sc = jnp.where(visible, sc, far_below)
            top = jnp.maximum(tops[u], jnp.max(sc, axis=1, keepdims=True))
            w = jnp.where(visible, jnp.exp(sc - top), 0.0)
            shrink = jnp.exp(tops[u] - top)
            sums[u] = sums[u] * shrink + jnp.sum(w, axis=1, keepdims=True)
            accs[u] = accs[u] * shrink + dot(w.astype(BF16), values)
            tops[u] = top
    for u in range(heads):
        att2[:, u * HD:(u + 1) * HD] = (accs[u] / sums[u]).astype(BF16)

    gather_wait(wso_all, ws, near)
    gather_wait(wso_all, ws, far)

    @pl.when(outer)
    def _():
        gather_wait(wso_all, ws, 2)

    f1 = {}
    for p in (3, 1, 2, 0):
        y2, m2 = at_place(p)
        there = pl.ds(pl.multiple_of(m2 * cols, cols), cols)
        fother[p] = dot(att2[...], wso_all[y2 * 2 + 1 - core, :, there]).astype(BF16)
        f1[p] = rcopy(fother.at[p], fcore.at[p], mate)
        fmine[p] = dot(att2[...], wso_all[y2 * 2 + core, :, there]).astype(BF16)
    f2 = {}
    for p in (3, 1, 2):
        f1[p].wait_recv()
        fsum[p - 1] = (fmine[p].astype(F32) + fcore[p].astype(F32)).astype(BF16)
        f2[p] = rcopy(fsum.at[p - 1], frs.at[p - 1], peer(p))
    f1[0].wait_recv()

    @pl.when(c == e)
    def _():
        for d in residual:
            d.wait_send()

    @pl.when(c != e)
    def _():
        residual[0].wait_recv()

    total = midown[...].astype(F32) + fmine[0].astype(F32) + fcore[0].astype(F32)
    for p in (1, 2, 3):
        f2[p].wait_recv()
        total = total + frs[p - 1].astype(F32)
    out[...] = total.astype(BF16)
    for condition, d in issued:
        if condition is None:
            d.wait_send()
        else:
            pl.when(condition)(d.wait_send)


def scratch_shapes(n, n_enc, tok, width, feats, slots, nbr_rows, pair_width, cols):
    shard = width // n
    half, rows = tok // 2, tok // 8
    return [
        ((n, tok, shard), BF16),
        ((n_enc * slots, nbr_rows, pair_width), BF16),
        ((n, tok, feats), BF16),
        ((n - 1, tok, feats), BF16),
        ((tok, HD), F32),
        ((n, tok, feats), BF16),
        ((n, feats, shard), BF16),
        ((n, tok, shard), BF16),
        ((n, half, shard), BF16),
        ((n, half, shard), BF16),
        ((3, n, rows, shard), BF16),
        ((n, tok, shard), BF16),
        ((n, 8, tok), F32),
        ((n - 1, 8, tok), F32),
        ((n, tok, 2 * feats), BF16),
        ((n - 1, tok, 2 * feats), BF16),
        ((tok, 2 * feats), BF16),
        ((n, tok, feats), BF16),
        ((n - 1, tok, feats), BF16),
        ((tok, feats), BF16),
        ((tok, feats), BF16),
        ((n, tok, 2 * feats), BF16),
        ((tok, cols), BF16),
        ((tok, feats), BF16),
        ((4, tok, cols), BF16),
        ((4, tok, cols), BF16),
        ((4, tok, cols), BF16),
        ((3, tok, cols), BF16),
        ((3, tok, cols), BF16),
    ]


def per_device_any(sizes, *args):
    n, n_enc, n_mp = sizes
    hidden_in, norm_gains, w_cross_query, w_cross_out, w_self_qkv, w_self_out, nbr_kv = args[:7]
    tok, width = hidden_in.shape
    feats = w_cross_query.shape[1]
    cols = width // (n_enc * n_mp)
    slots, nbr_rows, pair_width = nbr_kv.shape[3:]
    held = scratch_shapes(n, n_enc, tok, width, feats, slots, nbr_rows, pair_width, cols)
    need = sum(math.prod(shape) * jnp.dtype(kind).itemsize for shape, kind in held)
    if need > VMEM_GRANT // 2 or sizes != (4, 4, 2) or width != n * 2 * cols:
        return per_device(*args)
    copies = 128
    vmem = pl.BlockSpec(memory_space=pltpu.VMEM)
    smem = pl.BlockSpec(memory_space=pltpu.SMEM)
    return pl.pallas_call(
        block_kernel,
        out_shape=jax.ShapeDtypeStruct((tok, cols), BF16),
        in_specs=[vmem] * 7 + [smem] * 3,
        out_specs=vmem,
        scratch_shapes=[pltpu.VMEM(shape, kind) for shape, kind in held]
        + [pltpu.SemaphoreType.DMA((copies,)), pltpu.SemaphoreType.DMA((copies,))],
        compiler_params=pltpu.CompilerParams(
            collective_id=0, has_side_effects=True, vmem_limit_bytes=VMEM_GRANT
        ),
    )(
        hidden_in, norm_gains, w_cross_query, w_cross_out,
        w_self_qkv.reshape(w_self_qkv.shape[0], 3 * feats), w_self_out,
        nbr_kv[0, 0], *args[7:],
    )


def solution(mesh):
    in_specs = (
        P("ctx", None),
        P(),
        P("ctx", ("enc", "mp")),
        P(("enc", "mp"), "ctx"),
        P("ctx", None, ("enc", "mp")),
        P(("enc", "mp"), "ctx"),
        P("ctx", "enc", None, None, None, "mp"),
        P("ctx"),
        P("ctx", None),
        P(),
    )
    out_specs = P("ctx", ("enc", "mp"))
    sizes = (mesh.shape["ctx"], mesh.shape["enc"], mesh.shape["mp"])
    return jax.shard_map(
        functools.partial(per_device_any, sizes), mesh=mesh, in_specs=in_specs, out_specs=out_specs, check_vma=False
    )
```

```python
import functools
import math

import jax
import jax.numpy as jnp
from jax import lax
from jax.experimental import pallas as pl
from jax.experimental.pallas import tpu as pltpu
from jax.sharding import PartitionSpec as P

MESH = pl.DeviceIdType.MESH
VMEM_GRANT = 56 * 1024 * 1024
BF16 = jnp.bfloat16
F32 = jnp.float32

HD = 128
SPAN = 64


epsilon = 1e-05
far_below = -1e30


def rms_rows(row_values, gain_row):
    values = row_values.astype(jnp.float32)
    row_scale = lax.rsqrt(jnp.mean(values * values, axis=-1, keepdims=True) + epsilon)
    return (values * row_scale * gain_row).astype(jnp.bfloat16)


def token_places(order_table, first_row, row_count):
    tokens = first_row + jnp.arange(row_count, dtype=jnp.int32)
    blocks = tokens // SPAN
    matches = blocks[:, None] == jnp.arange(order_table.shape[0], dtype=jnp.int32)[None, :]
    placed = jnp.sum(jnp.where(matches, order_table[None, :], 0), axis=1)
    return placed * SPAN + tokens % SPAN


def per_device(
    hidden_in,
    norm_gains,
    w_cross_query,
    w_cross_out,
    w_self_qkv,
    w_self_out,
    nbr_kv,
    nbr_count,
    nbr_source,
    span_order,
):
    tok_rows, model_width = hidden_in.shape
    features = w_cross_query.shape[1]
    heads_here = features // HD
    groups = lax.axis_size(("enc", "mp"))
    share_width = model_width // groups
    group_index = lax.axis_index(("enc", "mp"))
    column = lax.axis_index("ctx")
    attn_scale = 1.0 / math.sqrt(HD)
    normed = rms_rows(hidden_in, norm_gains[0])
    columns_part = normed
    cross_query = jnp.dot(
        columns_part,
        lax.all_gather(w_cross_query, "ctx", axis=0, tiled=True),
        preferred_element_type=jnp.float32,
    ).astype(jnp.bfloat16)
    arrived = lax.all_to_all(nbr_kv[0, 0], "enc", split_axis=0, concat_axis=0, tiled=True)
    sources, slot_count, nbr_rows, pair_width = arrived.shape
    flattened = arrived.reshape(sources * slot_count, nbr_rows, pair_width)
    spans_here, per_span = nbr_source.shape
    chosen = nbr_source.reshape(-1)
    matches = (chosen[:, None] == jnp.arange(sources, dtype=jnp.int32)[None, :]).astype(jnp.int32)
    earlier = jnp.cumsum(matches, axis=0) - matches
    places = chosen * slot_count + jnp.sum(earlier * matches, axis=1)
    picked = jnp.take(flattened, places, axis=0)
    picked = picked.reshape(spans_here, per_span, nbr_rows, heads_here, 2, HD)
    nbr_keys = picked[:, :, :, :, 0, :]
    nbr_values = picked[:, :, :, :, 1, :]
    queries = cross_query.reshape(spans_here, tok_rows // spans_here, heads_here, HD)
    scores = (
        jnp.einsum("cqhd,cjrhd->chqjr", queries, nbr_keys, preferred_element_type=jnp.float32)
        * attn_scale
    )
    alive_mask = jnp.arange(per_span, dtype=jnp.int32)[None, :] < nbr_count[:, None]
    scores = jnp.where(alive_mask[:, None, None, :, None], scores, far_below)
    row_top = jnp.max(scores, axis=(3, 4), keepdims=True)
    weights_f = jnp.exp(scores - row_top)
    row_total = jnp.sum(weights_f, axis=(3, 4))
    mixed_heads = (
        jnp.einsum(
            "chqjr,cjrhd->chqd",
            weights_f.astype(jnp.bfloat16),
            nbr_values,
            preferred_element_type=jnp.float32,
        )
        / row_total[..., None]
    )
    cross_att = mixed_heads.transpose(0, 2, 1, 3).reshape(tok_rows, features).astype(jnp.bfloat16)
    cross_term = jnp.dot(
        cross_att,
        lax.all_gather(w_cross_out, "ctx", axis=1, tiled=True),
        preferred_element_type=jnp.float32,
    )
    summed = lax.psum(cross_term.astype(jnp.bfloat16), ("enc", "mp")).astype(jnp.float32)
    mid_full = (hidden_in.astype(jnp.float32) + summed).astype(jnp.bfloat16)
    mid_normed = rms_rows(mid_full, norm_gains[1])
    mid_share = lax.dynamic_slice_in_dim(mid_full, group_index * share_width, share_width, 1)
    shard_piece = lax.all_gather(w_self_qkv, "ctx", axis=0, tiled=True)
    columns_part = mid_normed
    projected = jnp.dot(
        columns_part,
        shard_piece.reshape(shard_piece.shape[0], 3 * features),
        preferred_element_type=jnp.float32,
    )
    projected = projected.astype(jnp.bfloat16).reshape(tok_rows, 3, heads_here, HD)
    self_query = projected[:, 0]
    keys_values = projected[:, 1:]
    query_places = token_places(span_order, column * tok_rows, tok_rows)
    shard_piece = lax.all_gather(keys_values, "ctx", axis=0, tiled=True)
    old_top = jnp.full((heads_here, tok_rows), far_below, jnp.float32)
    key_places = token_places(span_order, jnp.int32(0), shard_piece.shape[0])
    block_scores = (
        jnp.einsum(
            "qhd,khd->hqk", self_query, shard_piece[:, 0], preferred_element_type=jnp.float32
        )
        * attn_scale
    )
    visible = key_places[None, None, :] <= query_places[None, :, None]
    block_scores = jnp.where(visible, block_scores, far_below)
    new_top = jnp.maximum(old_top, jnp.max(block_scores, axis=2))
    block_weights = jnp.where(visible, jnp.exp(block_scores - new_top[..., None]), 0.0)
    new_total = jnp.sum(block_weights, axis=2)
    running = jnp.einsum(
        "hqk,khd->hqd",
        block_weights.astype(jnp.bfloat16),
        shard_piece[:, 1],
        preferred_element_type=jnp.float32,
    )
    self_att = (
        (running / new_total[..., None])
        .transpose(1, 0, 2)
        .reshape(tok_rows, features)
        .astype(jnp.bfloat16)
    )
    self_term = jnp.dot(
        self_att,
        lax.all_gather(w_self_out, "ctx", axis=1, tiled=True),
        preferred_element_type=jnp.float32,
    )
    out_share = lax.psum_scatter(
        self_term.astype(jnp.bfloat16), ("enc", "mp"), scatter_dimension=1, tiled=True
    ).astype(jnp.float32)
    return (mid_share.astype(jnp.float32) + out_share).astype(jnp.bfloat16)


def dot(a, b):
    return jnp.dot(a, b, preferred_element_type=F32)


def dot_t(a, b):
    return lax.dot_general(a, b, (((1,), (1,)), ((), ())), preferred_element_type=F32)


def block_kernel(
    hid_in, gains, wq_in, wco_in, wqkv_in, wso, nbr, cnt, nsrc, order, out,
    hid, wq, wco, wqkv, hid_all, nbr_all, qsend, qpart, rs0, att_all, wso_all, term, corebuf, cs, rsbuf, mid_all,
    sssend, sspart, kvsend, kvpart, kvrelay, q2send, q2part, q2relay, qbuf, kv_all, midown, att2, fother, fmine, fcore, fsum, frs,
    send_sems, recv_sems, local_sems,
):
    c, e, m = lax.axis_index("ctx"), lax.axis_index("enc"), lax.axis_index("mp")
    n = hid_all.shape[0]
    tok, width = hid.shape
    shard = width // n
    feats = wq.shape[1]
    heads = feats // HD
    slots = nbr.shape[1]
    n_enc = nbr.shape[0]
    rows = tok // 8
    half = tok // 2
    cols = out.shape[1]
    attn_scale = 1.0 / math.sqrt(HD)

    core, y = lax.rem(e, 2), e // 2
    mate = {"enc": e + 1 - 2 * core}
    place = y * 2 + m

    def at_place(p):
        y2 = 1 - y if p & 2 else y
        m2 = 1 - m if p & 1 else m
        return y2, m2

    def peer(p):
        y2, m2 = at_place(p)
        return {"enc": y2 * 2 + core, "mp": m2}

    def ctx_of(k):
        return lax.rem(c + k, n)

    def src_of(k):
        return lax.rem(c - k + n, n)

    near = 3 - 2 * (c // 2)
    far = 4 - near
    is_inner = lax.rem((c + 1) // 2, 2)
    is_outer = 1 - is_inner
    inner, outer = is_inner == 1, is_outer == 1
    turns = [0, is_inner * near + is_outer * 2, far, is_inner * 2 + is_outer * near]

    issued = []
    count = [0]

    def alloc(amount):
        count[0] += amount
        return count[0] - amount

    def describe(src, dst, device, send, recv):
        return pltpu.make_async_remote_copy(
            src_ref=src, dst_ref=dst, send_sem=send_sems.at[send], recv_sem=recv_sems.at[recv],
            device_id=device, device_id_type=MESH,
        )

    def rcopy(src, dst, device):
        i = alloc(1)
        d = describe(src, dst, device, i, i)
        d.start()
        issued.append((None, d))
        return d

    def gather_start(src, buf, base, part=slice(None)):
        def one(k):
            return describe(src, buf.at[c, part], {"ctx": ctx_of(k)}, base + k - 1, base + k - 1)

        last = one(near)
        for d in (one(2), one(far)):
            d.start()
            issued.append((None, d))

        @pl.when(inner)
        def _():
            last.start()

        issued.append((inner, last))

    def gather_wait(buf, base, k, part=slice(None)):
        block = buf.at[c, part]
        describe(block, block, {"ctx": ctx_of(1)}, base, base + k - 1).wait_recv()

    def gather_relay(buf, base, part=slice(None)):
        block = buf.at[src_of(2), part]
        d = describe(block, block, {"ctx": (c - 1) * 3}, base + 3, base + 2 * is_inner * (c - 1))
        issued.append((inner, d))

        @pl.when(inner)
        def _():
            d.start()

    def scatter_send(turn, send, part, relay, base):
        k = turns[turn]
        s = src_of(k)
        at = base + turn - 1
        direct = describe(send.at[s], part.at[k - 1], {"ctx": s}, at, base + k - 1)
        via = describe(send.at[s], relay, {"ctx": 1 + c // 3}, at, base + 3)
        if turn == 2:
            @pl.when(outer)
            def _():
                via.start()

            @pl.when(inner)
            def _():
                direct.start()
        elif turn == 3:
            pl.when(outer)(direct.start)
        else:
            direct.start()
        issued.append((None, direct))

    def scatter_merge(send, part, relay, base):
        k = turns[3]
        s = src_of(k)
        direct = describe(send.at[s], part.at[k - 1], {"ctx": s}, base + 2, base + k - 1)
        via = describe(send.at[s], relay, {"ctx": 1 + c // 3}, base + 2, base + 3)

        @pl.when(inner)
        def _():
            via.wait_recv()
            send[s] = (send[s].astype(F32) + relay[...].astype(F32)).astype(BF16)
            direct.start()

    def scatter_wait(part, base):
        def one(k):
            block = part.at[0]
            describe(block, block, {"ctx": ctx_of(1)}, base, base + k - 1).wait_recv()

        one(2)
        one(far)

        @pl.when(inner)
        def _():
            one(near)

        @pl.when(outer)
        def _():
            part[near - 1] = jnp.zeros(part.shape[1:], BF16)

    barrier = pltpu.get_barrier_semaphore()
    friends = [{"ctx": ctx_of(k)} for k in range(1, n)]
    friends += [{"enc": lax.rem(e + k, n_enc)} for k in range(1, n_enc)]
    friends += [peer(1), peer(3)]
    for f in friends:
        pl.semaphore_signal(barrier, inc=1, device_id=f, device_id_type=MESH)
    pl.semaphore_wait(barrier, len(friends))

    my_rows = pl.ds(pl.multiple_of(core * half + place * rows, rows), rows)
    my_half = pl.ds(pl.multiple_of(core * half, half), half)
    mate_half = pl.ds(pl.multiple_of((1 - core) * half, half), half)
    my_shard = pl.ds(pl.multiple_of(c * shard, shard), shard)

    a1 = {}
    for k in range(1, n):
        t = ctx_of(k)
        there = pl.ds(pl.multiple_of(t * shard, shard), shard)
        a1[k] = rcopy(hid_in.at[my_rows, there], hid_all.at[c, my_rows, :], {"ctx": t})
    def fetch(i, src, dst):
        d = pltpu.make_async_copy(src, dst, local_sems.at[i])
        d.start()
        return d

    got_shard = fetch(0, hid_in.at[:, my_shard], hid_all.at[c])
    got_wq = fetch(1, wq_in, wq)
    got_hid = fetch(2, hid_in, hid)
    got_nbr = fetch(3, nbr.at[e], nbr_all.at[pl.ds(e * slots, slots)])
    got_wco = fetch(4, wco_in, wco)
    got_wqkv = fetch(5, wqkv_in, wqkv)
    got_wso = fetch(6, wso, wso_all.at[c])
    nb = []
    for k in range(1, n_enc):
        f = lax.rem(e + k, n_enc)
        nb.append(rcopy(nbr.at[f], nbr_all.at[pl.ds(e * slots, slots)], {"enc": f}))
    gain0 = gains[0:1, my_shard]
    gain1 = gains[1:2, my_shard]

    def project_query(s):
        x = (hid_all[s].astype(F32) * gain0).astype(BF16)
        qsend[s] = dot(x, wq[...]).astype(BF16)

    a2 = {}
    for k in range(1, n):
        s = src_of(k)
        a1[k].wait_recv()
        for p in (3, 1, 2):
            block = hid_all.at[s, my_rows, :]
            a2[k, p] = rcopy(block, block, peer(p))
    ws = (alloc(4), alloc(4))
    deep = feats // 2
    gather_start(wso.at[0:deep], wso_all, ws[0], pl.ds(0, deep))
    got_shard.wait()
    got_wq.wait()
    project_query(c)
    got_hid.wait()
    squares = jnp.zeros((tok, 1), F32)
    for j in range(n):
        x = hid[:, j * shard:(j + 1) * shard].astype(F32)
        squares = squares + jnp.sum(x * x, axis=1, keepdims=True)
    rs0[...] = jnp.broadcast_to(lax.rsqrt(squares / width + epsilon), rs0.shape)
    a3 = {}
    for k in range(1, n):
        s = src_of(k)
        for p in (1, 2, 3):
            a2[k, p].wait_recv()
        block = hid_all.at[s, my_half, :]
        a3[k] = rcopy(block, block, mate)
    qs = []
    for k in range(1, n):
        s = src_of(k)
        a3[k].wait_recv()
        project_query(s)
        qs.append(rcopy(qsend.at[s], qpart.at[k - 1], {"ctx": s}))
    got_nbr.wait()
    for d in nb:
        d.wait_recv()
    for d in qs:
        d.wait_recv()
    q = qsend[c].astype(F32)
    for k in range(n - 1):
        q = q + qpart[k].astype(F32)
    q = (q * rs0[:, 0:1]).astype(BF16)

    per_span, spans = nsrc.shape
    lane = lax.broadcasted_iota(jnp.int32, (SPAN, per_span * SPAN), 1)
    for i in range(spans):
        kv = []
        for j in range(per_span):
            chosen = nsrc[j, i]
            rank = 0
            for i2 in range(i):
                for j2 in range(per_span):
                    rank = rank + jnp.where(nsrc[j2, i2] == chosen, 1, 0)
            kv.append(nbr_all[chosen * slots + rank])
        alive = lane < cnt[i] * SPAN
        for u in range(heads):
            lo = 2 * u * HD
            keys = jnp.concatenate([b[:, lo:lo + HD] for b in kv], axis=0)
            values = jnp.concatenate([b[:, lo + HD:lo + 2 * HD] for b in kv], axis=0)
            qi = q[i * SPAN:(i + 1) * SPAN, u * HD:(u + 1) * HD]
            sc = jnp.where(alive, dot_t(qi, keys) * attn_scale, far_below)
            w = jnp.exp(sc - jnp.max(sc, axis=1, keepdims=True))
            mixed = dot(w.astype(BF16), values) / jnp.sum(w, axis=1, keepdims=True)
            att_all[c, i * SPAN:(i + 1) * SPAN, u * HD:(u + 1) * HD] = mixed.astype(BF16)

    at = alloc(3)
    for k in range(1, n):
        d = describe(att_all.at[c], att_all.at[c], {"ctx": ctx_of(k)}, at + k - 1, at + k - 1)
        d.start()
        issued.append((None, d))
    gather_start(wso.at[deep:], wso_all, ws[1], pl.ds(deep, deep))

    @pl.when(inner)
    def _():
        gather_wait(wso_all, ws[0], 2, pl.ds(0, deep))

    gather_relay(wso_all, ws[0], pl.ds(0, deep))
    got_wco.wait()
    got_wqkv.wait()

    c2, c3, c4, c5, ssp = {}, {}, {}, {}, []
    kvb, q2b = alloc(4), alloc(4)

    def project_out(j):
        s = src_of(turns[j])
        if j:
            gather_wait(att_all, at, turns[j])
        term[s] = dot(att_all[s], wco[...]).astype(BF16)
        c2[j] = rcopy(term.at[s, mate_half, :], corebuf.at[s], mate)

    def pair_sum(j):
        s = src_of(turns[j])
        c2[j].wait_recv()
        cs[s] = (term[s, my_half, :].astype(F32) + corebuf[s].astype(F32)).astype(BF16)
        for p in (3, 1, 2):
            y2, m2 = at_place(p)
            theirs = pl.ds(pl.multiple_of((y2 * 2 + m2) * rows, rows), rows)
            c3[j, p] = rcopy(cs.at[s, theirs, :], rsbuf.at[p - 1, s], peer(p))

    def plane_sum(j):
        s = src_of(turns[j])
        total = hid_all[s, my_rows, :].astype(F32)
        total = total + cs[s, pl.ds(pl.multiple_of(place * rows, rows), rows), :].astype(F32)
        for p in (1, 2, 3):
            c3[j, p].wait_recv()
            total = total + rsbuf[p - 1, s].astype(F32)
        mid_all[s, my_rows, :] = total.astype(BF16)
        block = mid_all.at[s, my_rows, :]
        for p in (3, 1, 2):
            c4[j, p] = rcopy(block, block, peer(p))

    def plane_share(j):
        s = src_of(turns[j])
        for p in (1, 2, 3):
            c4[j, p].wait_recv()
        block = mid_all.at[s, my_half, :]
        c5[j] = rcopy(block, block, mate)

    def project_kv(j):
        s = src_of(turns[j])
        c5[j].wait_recv()
        x = mid_all[s].astype(F32)
        squares = jnp.sum(x * x, axis=1, keepdims=True)
        sssend[s] = jnp.broadcast_to(squares, (tok, HD)).T[0:8]
        x = (x * gain1).astype(BF16)
        kvsend[s, :, 0:feats] = dot(x, wqkv[1]).astype(BF16)
        kvsend[s, :, feats:] = dot(x, wqkv[2]).astype(BF16)
        if j:
            scatter_send(j, kvsend, kvpart, kvrelay, kvb)
        if j == 3:
            scatter_merge(kvsend, kvpart, kvrelay, kvb)

    stages = (project_out, pair_sum, plane_sum, plane_share, project_kv)
    for step in range(n + len(stages) - 1):
        for i in reversed(range(len(stages))):
            if 0 <= step - i < n:
                stages[i](step - i)
    for k in range(1, n):
        s = src_of(k)
        ssp.append(rcopy(sssend.at[s], sspart.at[k - 1], {"ctx": s}))
    for j in (1, 2, 3, 0):
        s = src_of(turns[j])
        x = (mid_all[s].astype(F32) * gain1).astype(BF16)
        q2send[s] = dot(x, wqkv[0]).astype(BF16)
        if j:
            scatter_send(j, q2send, q2part, q2relay, q2b)
    my_cols = pl.ds(pl.multiple_of(m * cols, cols), cols)

    def whole(send, part):
        total = send[c].astype(F32)
        for k in range(n - 1):
            total = total + part[k].astype(F32)
        return (total * row_scale).astype(BF16)

    for d in ssp:
        d.wait_recv()
    squares = sssend[c]
    for k in range(n - 1):
        squares = squares + sspart[k]
    squares = jnp.broadcast_to(squares[0:1], (HD, tok)).T[:, 0:1]
    row_scale = lax.rsqrt(squares / width + epsilon)
    scatter_wait(kvpart, kvb)
    kv_all[c] = whole(kvsend, kvpart)
    kvg = alloc(4)
    gather_start(kv_all.at[c], kv_all, kvg)

    scatter_merge(q2send, q2part, q2relay, q2b)

    @pl.when(inner)
    def _():
        gather_wait(wso_all, ws[1], 2, pl.ds(deep, deep))

    gather_relay(wso_all, ws[1], pl.ds(deep, deep))

    resid = alloc(3)
    residual = []
    for k in range(1, n):
        t = ctx_of(k)
        residual.append(
            describe(mid_all.at[t, :, my_cols], midown, {"ctx": t}, resid + k - 1, resid)
        )

    @pl.when(c == e)
    def _():
        for d in residual:
            d.start()
        midown[...] = mid_all[c, :, my_cols]

    scatter_wait(q2part, q2b)
    qbuf[...] = whole(q2send, q2part)

    def places(s, shape, axis):
        index = lax.broadcasted_iota(jnp.int32, shape, axis)
        first = s * (tok // SPAN)
        found = jnp.zeros(shape, jnp.int32)
        for b in range(tok // SPAN):
            found = jnp.where(index // SPAN == b, order[first + b], found)
        return found * SPAN + lax.rem(index, SPAN)

    query_places = places(c, (tok, 1), 0)
    tops = [jnp.full((tok, 1), far_below, F32) for _ in range(heads)]
    sums = [jnp.zeros((tok, 1), F32) for _ in range(heads)]
    accs = [jnp.zeros((tok, HD), F32) for _ in range(heads)]
    arrivals = (0, is_inner * 2 + is_outer * near, is_inner * near + is_outer * 2, far)
    for i, k in enumerate(arrivals):
        s = src_of(k)
        if i:
            gather_wait(kv_all, kvg, k)
        if i == 1:
            gather_relay(kv_all, kvg)
        visible = places(s, (1, tok), 1) <= query_places
        for u in range(heads):
            keys = kv_all[s, :, u * HD:(u + 1) * HD]
            values = kv_all[s, :, feats + u * HD:feats + (u + 1) * HD]
            sc = dot_t(qbuf[:, u * HD:(u + 1) * HD], keys) * attn_scale
            sc = jnp.where(visible, sc, far_below)
            top = jnp.maximum(tops[u], jnp.max(sc, axis=1, keepdims=True))
            w = jnp.where(visible, jnp.exp(sc - top), 0.0)
            shrink = jnp.exp(tops[u] - top)
            sums[u] = sums[u] * shrink + jnp.sum(w, axis=1, keepdims=True)
            accs[u] = accs[u] * shrink + dot(w.astype(BF16), values)
            tops[u] = top
    for u in range(heads):
        att2[:, u * HD:(u + 1) * HD] = (accs[u] / sums[u]).astype(BF16)

    got_wso.wait()
    for i in range(2):
        part = pl.ds(i * deep, deep)
        gather_wait(wso_all, ws[i], near, part)
        gather_wait(wso_all, ws[i], far, part)

        @pl.when(outer)
        def _():
            gather_wait(wso_all, ws[i], 2, part)

    f1 = {}
    for p in (3, 1, 2, 0):
        y2, m2 = at_place(p)
        there = pl.ds(pl.multiple_of(m2 * cols, cols), cols)
        fother[p] = dot(att2[...], wso_all[y2 * 2 + 1 - core, :, there]).astype(BF16)
        f1[p] = rcopy(fother.at[p], fcore.at[p], mate)
        fmine[p] = dot(att2[...], wso_all[y2 * 2 + core, :, there]).astype(BF16)
    f2 = {}
    for p in (3, 1, 2):
        f1[p].wait_recv()
        fsum[p - 1] = (fmine[p].astype(F32) + fcore[p].astype(F32)).astype(BF16)
        f2[p] = rcopy(fsum.at[p - 1], frs.at[p - 1], peer(p))
    f1[0].wait_recv()

    @pl.when(c == e)
    def _():
        for d in residual:
            d.wait_send()

    @pl.when(c != e)
    def _():
        residual[0].wait_recv()

    total = midown[...].astype(F32) + fmine[0].astype(F32) + fcore[0].astype(F32)
    for p in (1, 2, 3):
        f2[p].wait_recv()
        total = total + frs[p - 1].astype(F32)
    out[...] = total.astype(BF16)
    for condition, d in issued:
        if condition is None:
            d.wait_send()
        else:
            pl.when(condition)(d.wait_send)


def scratch_shapes(n, n_enc, tok, width, feats, slots, nbr_rows, pair_width, cols):
    shard = width // n
    half, rows = tok // 2, tok // 8
    return [
        ((tok, width), BF16),
        ((shard, feats), BF16),
        ((feats, shard), BF16),
        ((3, shard, feats), BF16),
        ((n, tok, shard), BF16),
        ((n_enc * slots, nbr_rows, pair_width), BF16),
        ((n, tok, feats), BF16),
        ((n - 1, tok, feats), BF16),
        ((tok, HD), F32),
        ((n, tok, feats), BF16),
        ((n, feats, shard), BF16),
        ((n, tok, shard), BF16),
        ((n, half, shard), BF16),
        ((n, half, shard), BF16),
        ((3, n, rows, shard), BF16),
        ((n, tok, shard), BF16),
        ((n, 8, tok), F32),
        ((n - 1, 8, tok), F32),
        ((n, tok, 2 * feats), BF16),
        ((n - 1, tok, 2 * feats), BF16),
        ((tok, 2 * feats), BF16),
        ((n, tok, feats), BF16),
        ((n - 1, tok, feats), BF16),
        ((tok, feats), BF16),
        ((tok, feats), BF16),
        ((n, tok, 2 * feats), BF16),
        ((tok, cols), BF16),
        ((tok, feats), BF16),
        ((4, tok, cols), BF16),
        ((4, tok, cols), BF16),
        ((4, tok, cols), BF16),
        ((3, tok, cols), BF16),
        ((3, tok, cols), BF16),
    ]


def per_device_any(sizes, *args):
    n, n_enc, n_mp = sizes
    hidden_in, norm_gains, w_cross_query, w_cross_out, w_self_qkv, w_self_out, nbr_kv = args[:7]
    tok, width = hidden_in.shape
    feats = w_cross_query.shape[1]
    cols = width // (n_enc * n_mp)
    slots, nbr_rows, pair_width = nbr_kv.shape[3:]
    held = scratch_shapes(n, n_enc, tok, width, feats, slots, nbr_rows, pair_width, cols)
    need = sum(math.prod(shape) * jnp.dtype(kind).itemsize for shape, kind in held)
    if need > VMEM_GRANT // 2 or sizes != (4, 4, 2) or width != n * 2 * cols:
        return per_device(*args)
    copies = 128
    vmem = pl.BlockSpec(memory_space=pltpu.VMEM)
    smem = pl.BlockSpec(memory_space=pltpu.SMEM)
    hbm = pl.BlockSpec(memory_space=pl.ANY)
    return pl.pallas_call(
        block_kernel,
        out_shape=jax.ShapeDtypeStruct((tok, cols), BF16),
        in_specs=[hbm, vmem, hbm, hbm, hbm, hbm, hbm] + [smem] * 3,
        out_specs=vmem,
        scratch_shapes=[pltpu.VMEM(shape, kind) for shape, kind in held]
        + [pltpu.SemaphoreType.DMA((copies,)), pltpu.SemaphoreType.DMA((copies,))]
        + [pltpu.SemaphoreType.DMA((8,))],
        compiler_params=pltpu.CompilerParams(
            collective_id=0, has_side_effects=True, vmem_limit_bytes=VMEM_GRANT
        ),
    )(
        hidden_in, norm_gains, w_cross_query, w_cross_out,
        jnp.transpose(w_self_qkv, (1, 0, 2)), w_self_out,
        nbr_kv[0, 0], args[7], args[8].T, args[9],
    )


def solution(mesh):
    in_specs = (
        P("ctx", None),
        P(),
        P("ctx", ("enc", "mp")),
        P(("enc", "mp"), "ctx"),
        P("ctx", None, ("enc", "mp")),
        P(("enc", "mp"), "ctx"),
        P("ctx", "enc", None, None, None, "mp"),
        P("ctx"),
        P("ctx", None),
        P(),
    )
    out_specs = P("ctx", ("enc", "mp"))
    sizes = (mesh.shape["ctx"], mesh.shape["enc"], mesh.shape["mp"])
    return jax.shard_map(
        functools.partial(per_device_any, sizes), mesh=mesh, in_specs=in_specs, out_specs=out_specs, check_vma=False
    )
```

```python
import functools
import math

import jax
import jax.numpy as jnp
from jax import lax
from jax.experimental import pallas as pl
from jax.experimental.pallas import tpu as pltpu
from jax.sharding import PartitionSpec as P

MESH = pl.DeviceIdType.MESH
VMEM_GRANT = 56 * 1024 * 1024
BF16 = jnp.bfloat16
F32 = jnp.float32

HD = 128
SPAN = 64


epsilon = 1e-05
far_below = -1e30


def rms_rows(row_values, gain_row):
    values = row_values.astype(jnp.float32)
    row_scale = lax.rsqrt(jnp.mean(values * values, axis=-1, keepdims=True) + epsilon)
    return (values * row_scale * gain_row).astype(jnp.bfloat16)


def token_places(order_table, first_row, row_count):
    tokens = first_row + jnp.arange(row_count, dtype=jnp.int32)
    blocks = tokens // SPAN
    matches = blocks[:, None] == jnp.arange(order_table.shape[0], dtype=jnp.int32)[None, :]
    placed = jnp.sum(jnp.where(matches, order_table[None, :], 0), axis=1)
    return placed * SPAN + tokens % SPAN


def per_device(
    hidden_in,
    norm_gains,
    w_cross_query,
    w_cross_out,
    w_self_qkv,
    w_self_out,
    nbr_kv,
    nbr_count,
    nbr_source,
    span_order,
):
    tok_rows, model_width = hidden_in.shape
    features = w_cross_query.shape[1]
    heads_here = features // HD
    groups = lax.axis_size(("enc", "mp"))
    share_width = model_width // groups
    group_index = lax.axis_index(("enc", "mp"))
    column = lax.axis_index("ctx")
    attn_scale = 1.0 / math.sqrt(HD)
    normed = rms_rows(hidden_in, norm_gains[0])
    columns_part = normed
    cross_query = jnp.dot(
        columns_part,
        lax.all_gather(w_cross_query, "ctx", axis=0, tiled=True),
        preferred_element_type=jnp.float32,
    ).astype(jnp.bfloat16)
    arrived = lax.all_to_all(nbr_kv[0, 0], "enc", split_axis=0, concat_axis=0, tiled=True)
    sources, slot_count, nbr_rows, pair_width = arrived.shape
    flattened = arrived.reshape(sources * slot_count, nbr_rows, pair_width)
    spans_here, per_span = nbr_source.shape
    chosen = nbr_source.reshape(-1)
    matches = (chosen[:, None] == jnp.arange(sources, dtype=jnp.int32)[None, :]).astype(jnp.int32)
    earlier = jnp.cumsum(matches, axis=0) - matches
    places = chosen * slot_count + jnp.sum(earlier * matches, axis=1)
    picked = jnp.take(flattened, places, axis=0)
    picked = picked.reshape(spans_here, per_span, nbr_rows, heads_here, 2, HD)
    nbr_keys = picked[:, :, :, :, 0, :]
    nbr_values = picked[:, :, :, :, 1, :]
    queries = cross_query.reshape(spans_here, tok_rows // spans_here, heads_here, HD)
    scores = (
        jnp.einsum("cqhd,cjrhd->chqjr", queries, nbr_keys, preferred_element_type=jnp.float32)
        * attn_scale
    )
    alive_mask = jnp.arange(per_span, dtype=jnp.int32)[None, :] < nbr_count[:, None]
    scores = jnp.where(alive_mask[:, None, None, :, None], scores, far_below)
    row_top = jnp.max(scores, axis=(3, 4), keepdims=True)
    weights_f = jnp.exp(scores - row_top)
    row_total = jnp.sum(weights_f, axis=(3, 4))
    mixed_heads = (
        jnp.einsum(
            "chqjr,cjrhd->chqd",
            weights_f.astype(jnp.bfloat16),
            nbr_values,
            preferred_element_type=jnp.float32,
        )
        / row_total[..., None]
    )
    cross_att = mixed_heads.transpose(0, 2, 1, 3).reshape(tok_rows, features).astype(jnp.bfloat16)
    cross_term = jnp.dot(
        cross_att,
        lax.all_gather(w_cross_out, "ctx", axis=1, tiled=True),
        preferred_element_type=jnp.float32,
    )
    summed = lax.psum(cross_term.astype(jnp.bfloat16), ("enc", "mp")).astype(jnp.float32)
    mid_full = (hidden_in.astype(jnp.float32) + summed).astype(jnp.bfloat16)
    mid_normed = rms_rows(mid_full, norm_gains[1])
    mid_share = lax.dynamic_slice_in_dim(mid_full, group_index * share_width, share_width, 1)
    shard_piece = lax.all_gather(w_self_qkv, "ctx", axis=0, tiled=True)
    columns_part = mid_normed
    projected = jnp.dot(
        columns_part,
        shard_piece.reshape(shard_piece.shape[0], 3 * features),
        preferred_element_type=jnp.float32,
    )
    projected = projected.astype(jnp.bfloat16).reshape(tok_rows, 3, heads_here, HD)
    self_query = projected[:, 0]
    keys_values = projected[:, 1:]
    query_places = token_places(span_order, column * tok_rows, tok_rows)
    shard_piece = lax.all_gather(keys_values, "ctx", axis=0, tiled=True)
    old_top = jnp.full((heads_here, tok_rows), far_below, jnp.float32)
    key_places = token_places(span_order, jnp.int32(0), shard_piece.shape[0])
    block_scores = (
        jnp.einsum(
            "qhd,khd->hqk", self_query, shard_piece[:, 0], preferred_element_type=jnp.float32
        )
        * attn_scale
    )
    visible = key_places[None, None, :] <= query_places[None, :, None]
    block_scores = jnp.where(visible, block_scores, far_below)
    new_top = jnp.maximum(old_top, jnp.max(block_scores, axis=2))
    block_weights = jnp.where(visible, jnp.exp(block_scores - new_top[..., None]), 0.0)
    new_total = jnp.sum(block_weights, axis=2)
    running = jnp.einsum(
        "hqk,khd->hqd",
        block_weights.astype(jnp.bfloat16),
        shard_piece[:, 1],
        preferred_element_type=jnp.float32,
    )
    self_att = (
        (running / new_total[..., None])
        .transpose(1, 0, 2)
        .reshape(tok_rows, features)
        .astype(jnp.bfloat16)
    )
    self_term = jnp.dot(
        self_att,
        lax.all_gather(w_self_out, "ctx", axis=1, tiled=True),
        preferred_element_type=jnp.float32,
    )
    out_share = lax.psum_scatter(
        self_term.astype(jnp.bfloat16), ("enc", "mp"), scatter_dimension=1, tiled=True
    ).astype(jnp.float32)
    return (mid_share.astype(jnp.float32) + out_share).astype(jnp.bfloat16)


def dot(a, b):
    return jnp.dot(a, b, preferred_element_type=F32)


def dot_t(a, b):
    return lax.dot_general(a, b, (((1,), (1,)), ((), ())), preferred_element_type=F32)


def block_kernel(
    hid_in, gains, wq_in, wco_in, wqkv_in, wso, nbr, cnt, nsrc, order, out,
    hid, wq, wco, wqkv, hid_all, nbr_all, qsend, qpart, rs0, att_all, wso_all, term, corebuf, cs, rsbuf, mid_all,
    sssend, sspart, kvsend, kvpart, kvrelay, q2send, q2part, q2relay, qbuf, kv_all, midown, att2, fother, fcore, fsum, frs,
    send_sems, recv_sems, local_sems,
):
    c, e, m = lax.axis_index("ctx"), lax.axis_index("enc"), lax.axis_index("mp")
    n = hid_all.shape[0]
    tok, width = hid.shape
    shard = width // n
    feats = wq.shape[1]
    heads = feats // HD
    slots = nbr.shape[1]
    n_enc = nbr.shape[0]
    rows = tok // 8
    half = tok // 2
    cols = out.shape[1]
    attn_scale = 1.0 / math.sqrt(HD)

    core, y = lax.rem(e, 2), e // 2
    mate = {"enc": e + 1 - 2 * core}
    place = y * 2 + m

    def at_place(p):
        y2 = 1 - y if p & 2 else y
        m2 = 1 - m if p & 1 else m
        return y2, m2

    def peer(p):
        y2, m2 = at_place(p)
        return {"enc": y2 * 2 + core, "mp": m2}

    def ctx_of(k):
        return lax.rem(c + k, n)

    def src_of(k):
        return lax.rem(c - k + n, n)

    near = 3 - 2 * (c // 2)
    far = 4 - near
    is_inner = lax.rem((c + 1) // 2, 2)
    is_outer = 1 - is_inner
    inner, outer = is_inner == 1, is_outer == 1
    turns = [0, is_inner * near + is_outer * 2, far, is_inner * 2 + is_outer * near]

    issued = []
    count = [0]

    def alloc(amount):
        count[0] += amount
        return count[0] - amount

    def describe(src, dst, device, send, recv):
        return pltpu.make_async_remote_copy(
            src_ref=src, dst_ref=dst, send_sem=send_sems.at[send], recv_sem=recv_sems.at[recv],
            device_id=device, device_id_type=MESH,
        )

    def rcopy(src, dst, device):
        i = alloc(1)
        d = describe(src, dst, device, i, i)
        d.start()
        issued.append((None, d))
        return d

    def gather_start(src, buf, base, part=slice(None)):
        def one(k):
            return describe(src, buf.at[c, part], {"ctx": ctx_of(k)}, base + k - 1, base + k - 1)

        last = one(near)
        for d in (one(2), one(far)):
            d.start()
            issued.append((None, d))

        @pl.when(inner)
        def _():
            last.start()

        issued.append((inner, last))

    def gather_wait(buf, base, k, part=slice(None)):
        block = buf.at[c, part]
        describe(block, block, {"ctx": ctx_of(1)}, base, base + k - 1).wait_recv()

    def gather_relay(buf, base, part=slice(None)):
        block = buf.at[src_of(2), part]
        d = describe(block, block, {"ctx": (c - 1) * 3}, base + 3, base + 2 * is_inner * (c - 1))
        issued.append((inner, d))

        @pl.when(inner)
        def _():
            d.start()

    def scatter_send(turn, send, part, relay, base):
        k = turns[turn]
        s = src_of(k)
        at = base + turn - 1
        direct = describe(send.at[s], part.at[k - 1], {"ctx": s}, at, base + k - 1)
        via = describe(send.at[s], relay, {"ctx": 1 + c // 3}, at, base + 3)
        if turn == 2:
            @pl.when(outer)
            def _():
                via.start()

            @pl.when(inner)
            def _():
                direct.start()
        elif turn == 3:
            pl.when(outer)(direct.start)
        else:
            direct.start()
        issued.append((None, direct))

    def scatter_merge(send, part, relay, base):
        k = turns[3]
        s = src_of(k)
        direct = describe(send.at[s], part.at[k - 1], {"ctx": s}, base + 2, base + k - 1)
        via = describe(send.at[s], relay, {"ctx": 1 + c // 3}, base + 2, base + 3)

        @pl.when(inner)
        def _():
            via.wait_recv()
            send[s] = (send[s].astype(F32) + relay[...].astype(F32)).astype(BF16)
            direct.start()

    def scatter_wait(part, base):
        def one(k):
            block = part.at[0]
            describe(block, block, {"ctx": ctx_of(1)}, base, base + k - 1).wait_recv()

        one(2)
        one(far)

        @pl.when(inner)
        def _():
            one(near)

        @pl.when(outer)
        def _():
            part[near - 1] = jnp.zeros(part.shape[1:], BF16)

    barrier = pltpu.get_barrier_semaphore()
    friends = [{"ctx": ctx_of(k)} for k in range(1, n)]
    friends += [{"enc": lax.rem(e + k, n_enc)} for k in range(1, n_enc)]
    friends += [peer(1), peer(3)]
    for f in friends:
        pl.semaphore_signal(barrier, inc=1, device_id=f, device_id_type=MESH)
    pl.semaphore_wait(barrier, len(friends))

    my_rows = pl.ds(pl.multiple_of(core * half + place * rows, rows), rows)
    my_half = pl.ds(pl.multiple_of(core * half, half), half)
    mate_half = pl.ds(pl.multiple_of((1 - core) * half, half), half)
    my_shard = pl.ds(pl.multiple_of(c * shard, shard), shard)

    a1 = alloc(3)
    for k in range(1, n):
        t = ctx_of(k)
        there = pl.ds(pl.multiple_of(t * shard, shard), shard)
        d = describe(
            hid_in.at[my_rows, there], hid_all.at[c, my_rows, :], {"ctx": t}, a1 + k - 1, a1 + k - 1
        )
        d.start()
        issued.append((None, d))
    nearest = {1: near, 2: is_inner * far + is_outer * 2, 3: is_inner * 2 + is_outer * far}
    def fetch(i, src, dst):
        d = pltpu.make_async_copy(src, dst, local_sems.at[i])
        d.start()
        return d

    got_shard = fetch(0, hid_in.at[:, my_shard], hid_all.at[c])
    got_wq = fetch(1, wq_in, wq)
    got_hid = fetch(2, hid_in, hid)
    got_nbr = fetch(3, nbr.at[e], nbr_all.at[pl.ds(e * slots, slots)])
    got_wco = fetch(4, wco_in, wco)
    got_wqkv = fetch(5, wqkv_in, wqkv)
    got_wso = fetch(6, wso, wso_all.at[c])
    nb = []
    for k in range(1, n_enc):
        f = lax.rem(e + k, n_enc)
        nb.append(rcopy(nbr.at[f], nbr_all.at[pl.ds(e * slots, slots)], {"enc": f}))
    gain0 = gains[0:1, my_shard]
    gain1 = gains[1:2, my_shard]

    def project_query(s):
        x = (hid_all[s].astype(F32) * gain0).astype(BF16)
        qsend[s] = dot(x, wq[...]).astype(BF16)

    a2 = {}
    for k in range(1, n):
        s = src_of(nearest[k])
        gather_wait(hid_all, a1, nearest[k], my_rows)
        for p in (3, 1, 2):
            block = hid_all.at[s, my_rows, :]
            a2[k, p] = rcopy(block, block, peer(p))
    ws = (alloc(4), alloc(4))
    deep = feats // 2
    gather_start(wso.at[0:deep], wso_all, ws[0], pl.ds(0, deep))
    got_shard.wait()
    got_wq.wait()
    project_query(c)
    got_hid.wait()
    squares = jnp.zeros((tok, 1), F32)
    for j in range(n):
        x = hid[:, j * shard:(j + 1) * shard].astype(F32)
        squares = squares + jnp.sum(x * x, axis=1, keepdims=True)
    rs0[...] = jnp.broadcast_to(lax.rsqrt(squares / width + epsilon), rs0.shape)
    a3 = {}
    for k in range(1, n):
        s = src_of(nearest[k])
        for p in (1, 2, 3):
            a2[k, p].wait_recv()
        block = hid_all.at[s, my_half, :]
        a3[k] = rcopy(block, block, mate)
    qs = alloc(3)
    for j in range(1, n):
        k = nearest[j]
        s = src_of(k)
        a3[j].wait_recv()
        project_query(s)
        d = describe(qsend.at[s], qpart.at[k - 1], {"ctx": s}, qs + j - 1, qs + k - 1)
        d.start()
        issued.append((None, d))
    got_nbr.wait()
    for d in nb:
        d.wait_recv()
    for k in range(1, n):
        gather_wait(qsend, qs, k)
    q = qsend[c].astype(F32)
    for k in range(n - 1):
        q = q + qpart[k].astype(F32)
    q = (q * rs0[:, 0:1]).astype(BF16)

    per_span, spans = nsrc.shape
    lane = lax.broadcasted_iota(jnp.int32, (SPAN, per_span * SPAN), 1)
    blocks = []
    for i in range(spans):
        kv = []
        for j in range(per_span):
            chosen = nsrc[j, i]
            rank = 0
            for i2 in range(i):
                for j2 in range(per_span):
                    rank = rank + jnp.where(nsrc[j2, i2] == chosen, 1, 0)
            kv.append(nbr_all[chosen * slots + rank])
        blocks.append(jnp.concatenate(kv, axis=0))
    for u in range(heads):
        lo = 2 * u * HD
        sc = []
        for i in range(spans):
            qi = q[i * SPAN:(i + 1) * SPAN, u * HD:(u + 1) * HD]
            si = dot_t(qi, blocks[i][:, lo:lo + HD]) * attn_scale
            sc.append(jnp.where(lane < cnt[i] * SPAN, si, far_below))
        sc = jnp.concatenate(sc, axis=0)
        w = jnp.exp(sc - jnp.max(sc, axis=1, keepdims=True))
        total = jnp.sum(w, axis=1, keepdims=True)
        w = w.astype(BF16)
        mixed = [
            dot(w[i * SPAN:(i + 1) * SPAN], blocks[i][:, lo + HD:lo + 2 * HD])
            for i in range(spans)
        ]
        mixed = jnp.concatenate(mixed, axis=0) / total
        att_all[c, :, u * HD:(u + 1) * HD] = mixed.astype(BF16)

    at = alloc(3)
    for k in range(1, n):
        d = describe(att_all.at[c], att_all.at[c], {"ctx": ctx_of(k)}, at + k - 1, at + k - 1)
        d.start()
        issued.append((None, d))
    gather_start(wso.at[deep:], wso_all, ws[1], pl.ds(deep, deep))

    @pl.when(inner)
    def _():
        gather_wait(wso_all, ws[0], 2, pl.ds(0, deep))

    gather_relay(wso_all, ws[0], pl.ds(0, deep))
    got_wco.wait()
    got_wqkv.wait()

    c2, c3, c4, c5, ssp = {}, {}, {}, {}, []
    kvb, q2b = alloc(4), alloc(4)

    def project_out(j):
        s = src_of(turns[j])
        if j:
            gather_wait(att_all, at, turns[j])
        term[s] = dot(att_all[s], wco[...]).astype(BF16)
        c2[j] = rcopy(term.at[s, mate_half, :], corebuf.at[s], mate)

    def pair_sum(j):
        s = src_of(turns[j])
        c2[j].wait_recv()
        cs[s] = (term[s, my_half, :].astype(F32) + corebuf[s].astype(F32)).astype(BF16)
        for p in (3, 1, 2):
            y2, m2 = at_place(p)
            theirs = pl.ds(pl.multiple_of((y2 * 2 + m2) * rows, rows), rows)
            c3[j, p] = rcopy(cs.at[s, theirs, :], rsbuf.at[p - 1, s], peer(p))

    def plane_sum(j):
        s = src_of(turns[j])
        total = hid_all[s, my_rows, :].astype(F32)
        total = total + cs[s, pl.ds(pl.multiple_of(place * rows, rows), rows), :].astype(F32)
        for p in (1, 2, 3):
            c3[j, p].wait_recv()
            total = total + rsbuf[p - 1, s].astype(F32)
        mid_all[s, my_rows, :] = total.astype(BF16)
        block = mid_all.at[s, my_rows, :]
        for p in (3, 1, 2):
            c4[j, p] = rcopy(block, block, peer(p))

    def plane_share(j):
        s = src_of(turns[j])
        for p in (1, 2, 3):
            c4[j, p].wait_recv()
        block = mid_all.at[s, my_half, :]
        c5[j] = rcopy(block, block, mate)

    def project_kv(j):
        s = src_of(turns[j])
        c5[j].wait_recv()
        x = mid_all[s].astype(F32)
        squares = jnp.sum(x * x, axis=1, keepdims=True)
        sssend[s] = jnp.broadcast_to(squares, (tok, HD)).T[0:8]
        x = (x * gain1).astype(BF16)
        kvsend[s, :, 0:feats] = dot(x, wqkv[1]).astype(BF16)
        kvsend[s, :, feats:] = dot(x, wqkv[2]).astype(BF16)
        if j:
            scatter_send(j, kvsend, kvpart, kvrelay, kvb)
        if j == 3:
            scatter_merge(kvsend, kvpart, kvrelay, kvb)

    stages = (project_out, pair_sum, plane_sum, plane_share, project_kv)
    for step in range(n + len(stages) - 1):
        for i in reversed(range(len(stages))):
            if 0 <= step - i < n:
                stages[i](step - i)
    for k in range(1, n):
        s = src_of(k)
        ssp.append(rcopy(sssend.at[s], sspart.at[k - 1], {"ctx": s}))
    for j in (1, 2, 3, 0):
        s = src_of(turns[j])
        x = (mid_all[s].astype(F32) * gain1).astype(BF16)
        q2send[s] = dot(x, wqkv[0]).astype(BF16)
        if j:
            scatter_send(j, q2send, q2part, q2relay, q2b)
    my_cols = pl.ds(pl.multiple_of(m * cols, cols), cols)

    def whole(send, part):
        total = send[c].astype(F32)
        for k in range(n - 1):
            total = total + part[k].astype(F32)
        return (total * row_scale).astype(BF16)

    for d in ssp:
        d.wait_recv()
    squares = sssend[c]
    for k in range(n - 1):
        squares = squares + sspart[k]
    squares = jnp.broadcast_to(squares[0:1], (HD, tok)).T[:, 0:1]
    row_scale = lax.rsqrt(squares / width + epsilon)
    scatter_wait(kvpart, kvb)
    kv_all[c] = whole(kvsend, kvpart)
    kvg = alloc(4)
    gather_start(kv_all.at[c], kv_all, kvg)

    scatter_merge(q2send, q2part, q2relay, q2b)

    @pl.when(inner)
    def _():
        gather_wait(wso_all, ws[1], 2, pl.ds(deep, deep))

    gather_relay(wso_all, ws[1], pl.ds(deep, deep))

    resid = alloc(3)
    residual = []
    for k in range(1, n):
        t = ctx_of(k)
        residual.append(
            describe(mid_all.at[t, :, my_cols], midown, {"ctx": t}, resid + k - 1, resid)
        )

    @pl.when(c == e)
    def _():
        for d in residual:
            d.start()
        midown[...] = mid_all[c, :, my_cols]

    scatter_wait(q2part, q2b)
    qbuf[...] = whole(q2send, q2part)

    def places(s, shape, axis):
        index = lax.broadcasted_iota(jnp.int32, shape, axis)
        first = s * (tok // SPAN)
        found = jnp.zeros(shape, jnp.int32)
        for b in range(tok // SPAN):
            found = jnp.where(index // SPAN == b, order[first + b], found)
        return found * SPAN + lax.rem(index, SPAN)

    query_places = places(c, (tok, 1), 0)
    tops = [jnp.full((tok, 1), far_below, F32) for _ in range(heads)]
    sums = [jnp.zeros((tok, 1), F32) for _ in range(heads)]
    accs = [jnp.zeros((tok, HD), F32) for _ in range(heads)]
    arrivals = (0, is_inner * 2 + is_outer * near, is_inner * near + is_outer * 2, far)
    for i, k in enumerate(arrivals):
        s = src_of(k)
        if i:
            gather_wait(kv_all, kvg, k)
        if i == 1:
            gather_relay(kv_all, kvg)
        visible = places(s, (1, tok), 1) <= query_places
        for u in range(heads):
            keys = kv_all[s, :, u * HD:(u + 1) * HD]
            values = kv_all[s, :, feats + u * HD:feats + (u + 1) * HD]
            sc = dot_t(qbuf[:, u * HD:(u + 1) * HD], keys) * attn_scale
            sc = jnp.where(visible, sc, far_below)
            top = jnp.maximum(tops[u], jnp.max(sc, axis=1, keepdims=True))
            w = jnp.where(visible, jnp.exp(sc - top), 0.0)
            shrink = jnp.exp(tops[u] - top)
            sums[u] = sums[u] * shrink + jnp.sum(w, axis=1, keepdims=True)
            accs[u] = accs[u] * shrink + dot(w.astype(BF16), values)
            tops[u] = top
    for u in range(heads):
        att2[:, u * HD:(u + 1) * HD] = (accs[u] / sums[u]).astype(BF16)

    got_wso.wait()
    for i in range(2):
        part = pl.ds(i * deep, deep)
        gather_wait(wso_all, ws[i], near, part)
        gather_wait(wso_all, ws[i], far, part)

        @pl.when(outer)
        def _():
            gather_wait(wso_all, ws[i], 2, part)

    f1, f2 = {}, {}

    def out_term(p, which):
        y2, m2 = at_place(p)
        there = pl.ds(pl.multiple_of(m2 * cols, cols), cols)
        return dot(att2[...], wso_all[y2 * 2 + which, :, there])

    def to_mate(p):
        fother[p] = out_term(p, 1 - core).astype(BF16)
        f1[p] = rcopy(fother.at[p], fcore.at[p], mate)

    for p in (3, 1, 2):
        to_mate(p)
    for p in (3, 1, 2):
        mine = out_term(p, core)
        f1[p].wait_recv()
        fsum[p - 1] = (mine + fcore[p].astype(F32)).astype(BF16)
        f2[p] = rcopy(fsum.at[p - 1], frs.at[p - 1], peer(p))
    to_mate(0)
    mine = out_term(0, core)
    f1[0].wait_recv()

    @pl.when(c == e)
    def _():
        for d in residual:
            d.wait_send()

    @pl.when(c != e)
    def _():
        residual[0].wait_recv()

    total = midown[...].astype(F32) + mine + fcore[0].astype(F32)
    for p in (1, 2, 3):
        f2[p].wait_recv()
        total = total + frs[p - 1].astype(F32)
    out[...] = total.astype(BF16)
    for condition, d in issued:
        if condition is None:
            d.wait_send()
        else:
            pl.when(condition)(d.wait_send)


def scratch_shapes(n, n_enc, tok, width, feats, slots, nbr_rows, pair_width, cols):
    shard = width // n
    half, rows = tok // 2, tok // 8
    return [
        ((tok, width), BF16),
        ((shard, feats), BF16),
        ((feats, shard), BF16),
        ((3, shard, feats), BF16),
        ((n, tok, shard), BF16),
        ((n_enc * slots, nbr_rows, pair_width), BF16),
        ((n, tok, feats), BF16),
        ((n - 1, tok, feats), BF16),
        ((tok, HD), F32),
        ((n, tok, feats), BF16),
        ((n, feats, shard), BF16),
        ((n, tok, shard), BF16),
        ((n, half, shard), BF16),
        ((n, half, shard), BF16),
        ((3, n, rows, shard), BF16),
        ((n, tok, shard), BF16),
        ((n, 8, tok), F32),
        ((n - 1, 8, tok), F32),
        ((n, tok, 2 * feats), BF16),
        ((n - 1, tok, 2 * feats), BF16),
        ((tok, 2 * feats), BF16),
        ((n, tok, feats), BF16),
        ((n - 1, tok, feats), BF16),
        ((tok, feats), BF16),
        ((tok, feats), BF16),
        ((n, tok, 2 * feats), BF16),
        ((tok, cols), BF16),
        ((tok, feats), BF16),
        ((4, tok, cols), BF16),
        ((4, tok, cols), BF16),
        ((3, tok, cols), BF16),
        ((3, tok, cols), BF16),
    ]


def per_device_any(sizes, *args):
    n, n_enc, n_mp = sizes
    hidden_in, norm_gains, w_cross_query, w_cross_out, w_self_qkv, w_self_out, nbr_kv = args[:7]
    tok, width = hidden_in.shape
    feats = w_cross_query.shape[1]
    cols = width // (n_enc * n_mp)
    slots, nbr_rows, pair_width = nbr_kv.shape[3:]
    held = scratch_shapes(n, n_enc, tok, width, feats, slots, nbr_rows, pair_width, cols)
    need = sum(math.prod(shape) * jnp.dtype(kind).itemsize for shape, kind in held)
    if need > VMEM_GRANT // 2 or sizes != (4, 4, 2) or width != n * 2 * cols:
        return per_device(*args)
    copies = 128
    vmem = pl.BlockSpec(memory_space=pltpu.VMEM)
    smem = pl.BlockSpec(memory_space=pltpu.SMEM)
    hbm = pl.BlockSpec(memory_space=pl.ANY)
    return pl.pallas_call(
        block_kernel,
        out_shape=jax.ShapeDtypeStruct((tok, cols), BF16),
        in_specs=[hbm, vmem, hbm, hbm, hbm, hbm, hbm] + [smem] * 3,
        out_specs=vmem,
        scratch_shapes=[pltpu.VMEM(shape, kind) for shape, kind in held]
        + [pltpu.SemaphoreType.DMA((copies,)), pltpu.SemaphoreType.DMA((copies,))]
        + [pltpu.SemaphoreType.DMA((8,))],
        compiler_params=pltpu.CompilerParams(
            collective_id=0, has_side_effects=True, vmem_limit_bytes=VMEM_GRANT
        ),
    )(
        hidden_in, norm_gains, w_cross_query, w_cross_out,
        jnp.transpose(w_self_qkv, (1, 0, 2)), w_self_out,
        nbr_kv[0, 0], args[7], args[8].T, args[9],
    )


def solution(mesh):
    in_specs = (
        P("ctx", None),
        P(),
        P("ctx", ("enc", "mp")),
        P(("enc", "mp"), "ctx"),
        P("ctx", None, ("enc", "mp")),
        P(("enc", "mp"), "ctx"),
        P("ctx", "enc", None, None, None, "mp"),
        P("ctx"),
        P("ctx", None),
        P(),
    )
    out_specs = P("ctx", ("enc", "mp"))
    sizes = (mesh.shape["ctx"], mesh.shape["enc"], mesh.shape["mp"])
    return jax.shard_map(
        functools.partial(per_device_any, sizes), mesh=mesh, in_specs=in_specs, out_specs=out_specs, check_vma=False
    )
```

```python
import functools
import math

import jax
import jax.numpy as jnp
from jax import lax
from jax.experimental import pallas as pl
from jax.experimental.pallas import tpu as pltpu
from jax.sharding import PartitionSpec as P

MESH = pl.DeviceIdType.MESH
VMEM_GRANT = 56 * 1024 * 1024
BF16 = jnp.bfloat16
F32 = jnp.float32

HD = 128
SPAN = 64


epsilon = 1e-05
far_below = -1e30


def rms_rows(row_values, gain_row):
    values = row_values.astype(jnp.float32)
    row_scale = lax.rsqrt(jnp.mean(values * values, axis=-1, keepdims=True) + epsilon)
    return (values * row_scale * gain_row).astype(jnp.bfloat16)


def token_places(order_table, first_row, row_count):
    tokens = first_row + jnp.arange(row_count, dtype=jnp.int32)
    blocks = tokens // SPAN
    matches = blocks[:, None] == jnp.arange(order_table.shape[0], dtype=jnp.int32)[None, :]
    placed = jnp.sum(jnp.where(matches, order_table[None, :], 0), axis=1)
    return placed * SPAN + tokens % SPAN


def per_device(
    hidden_in,
    norm_gains,
    w_cross_query,
    w_cross_out,
    w_self_qkv,
    w_self_out,
    nbr_kv,
    nbr_count,
    nbr_source,
    span_order,
):
    tok_rows, model_width = hidden_in.shape
    features = w_cross_query.shape[1]
    heads_here = features // HD
    groups = lax.axis_size(("enc", "mp"))
    share_width = model_width // groups
    group_index = lax.axis_index(("enc", "mp"))
    column = lax.axis_index("ctx")
    attn_scale = 1.0 / math.sqrt(HD)
    normed = rms_rows(hidden_in, norm_gains[0])
    columns_part = normed
    cross_query = jnp.dot(
        columns_part,
        lax.all_gather(w_cross_query, "ctx", axis=0, tiled=True),
        preferred_element_type=jnp.float32,
    ).astype(jnp.bfloat16)
    arrived = lax.all_to_all(nbr_kv[0, 0], "enc", split_axis=0, concat_axis=0, tiled=True)
    sources, slot_count, nbr_rows, pair_width = arrived.shape
    flattened = arrived.reshape(sources * slot_count, nbr_rows, pair_width)
    spans_here, per_span = nbr_source.shape
    chosen = nbr_source.reshape(-1)
    matches = (chosen[:, None] == jnp.arange(sources, dtype=jnp.int32)[None, :]).astype(jnp.int32)
    earlier = jnp.cumsum(matches, axis=0) - matches
    places = chosen * slot_count + jnp.sum(earlier * matches, axis=1)
    picked = jnp.take(flattened, places, axis=0)
    picked = picked.reshape(spans_here, per_span, nbr_rows, heads_here, 2, HD)
    nbr_keys = picked[:, :, :, :, 0, :]
    nbr_values = picked[:, :, :, :, 1, :]
    queries = cross_query.reshape(spans_here, tok_rows // spans_here, heads_here, HD)
    scores = (
        jnp.einsum("cqhd,cjrhd->chqjr", queries, nbr_keys, preferred_element_type=jnp.float32)
        * attn_scale
    )
    alive_mask = jnp.arange(per_span, dtype=jnp.int32)[None, :] < nbr_count[:, None]
    scores = jnp.where(alive_mask[:, None, None, :, None], scores, far_below)
    row_top = jnp.max(scores, axis=(3, 4), keepdims=True)
    weights_f = jnp.exp(scores - row_top)
    row_total = jnp.sum(weights_f, axis=(3, 4))
    mixed_heads = (
        jnp.einsum(
            "chqjr,cjrhd->chqd",
            weights_f.astype(jnp.bfloat16),
            nbr_values,
            preferred_element_type=jnp.float32,
        )
        / row_total[..., None]
    )
    cross_att = mixed_heads.transpose(0, 2, 1, 3).reshape(tok_rows, features).astype(jnp.bfloat16)
    cross_term = jnp.dot(
        cross_att,
        lax.all_gather(w_cross_out, "ctx", axis=1, tiled=True),
        preferred_element_type=jnp.float32,
    )
    summed = lax.psum(cross_term.astype(jnp.bfloat16), ("enc", "mp")).astype(jnp.float32)
    mid_full = (hidden_in.astype(jnp.float32) + summed).astype(jnp.bfloat16)
    mid_normed = rms_rows(mid_full, norm_gains[1])
    mid_share = lax.dynamic_slice_in_dim(mid_full, group_index * share_width, share_width, 1)
    shard_piece = lax.all_gather(w_self_qkv, "ctx", axis=0, tiled=True)
    columns_part = mid_normed
    projected = jnp.dot(
        columns_part,
        shard_piece.reshape(shard_piece.shape[0], 3 * features),
        preferred_element_type=jnp.float32,
    )
    projected = projected.astype(jnp.bfloat16).reshape(tok_rows, 3, heads_here, HD)
    self_query = projected[:, 0]
    keys_values = projected[:, 1:]
    query_places = token_places(span_order, column * tok_rows, tok_rows)
    shard_piece = lax.all_gather(keys_values, "ctx", axis=0, tiled=True)
    old_top = jnp.full((heads_here, tok_rows), far_below, jnp.float32)
    key_places = token_places(span_order, jnp.int32(0), shard_piece.shape[0])
    block_scores = (
        jnp.einsum(
            "qhd,khd->hqk", self_query, shard_piece[:, 0], preferred_element_type=jnp.float32
        )
        * attn_scale
    )
    visible = key_places[None, None, :] <= query_places[None, :, None]
    block_scores = jnp.where(visible, block_scores, far_below)
    new_top = jnp.maximum(old_top, jnp.max(block_scores, axis=2))
    block_weights = jnp.where(visible, jnp.exp(block_scores - new_top[..., None]), 0.0)
    new_total = jnp.sum(block_weights, axis=2)
    running = jnp.einsum(
        "hqk,khd->hqd",
        block_weights.astype(jnp.bfloat16),
        shard_piece[:, 1],
        preferred_element_type=jnp.float32,
    )
    self_att = (
        (running / new_total[..., None])
        .transpose(1, 0, 2)
        .reshape(tok_rows, features)
        .astype(jnp.bfloat16)
    )
    self_term = jnp.dot(
        self_att,
        lax.all_gather(w_self_out, "ctx", axis=1, tiled=True),
        preferred_element_type=jnp.float32,
    )
    out_share = lax.psum_scatter(
        self_term.astype(jnp.bfloat16), ("enc", "mp"), scatter_dimension=1, tiled=True
    ).astype(jnp.float32)
    return (mid_share.astype(jnp.float32) + out_share).astype(jnp.bfloat16)


def dot(a, b):
    return jnp.dot(a, b, preferred_element_type=F32)


def dot_t(a, b):
    return lax.dot_general(a, b, (((1,), (1,)), ((), ())), preferred_element_type=F32)


def block_kernel(
    hid_in, gains, wq_in, wco_in, wqkv_in, wso, nbr, cnt, nsrc, order, out,
    hid, wq, wco, wqkv, hid_all, nbr_all, qsend, qpart, rs0, att_all, wso_all, term, corebuf, cs, rsbuf, mid_all,
    sssend, sspart, kvsend, kvpart, kvrelay, q2send, q2part, q2relay, qbuf, kv_all, midown, att2, fother, fcore, fsum, frs,
    send_sems, recv_sems, local_sems,
):
    c, e, m = lax.axis_index("ctx"), lax.axis_index("enc"), lax.axis_index("mp")
    n = hid_all.shape[0]
    tok, width = hid.shape
    shard = width // n
    feats = wq.shape[1]
    heads = feats // HD
    slots = nbr.shape[1]
    n_enc = nbr.shape[0]
    rows = tok // 8
    half = tok // 2
    cols = out.shape[1]
    attn_scale = 1.0 / math.sqrt(HD)

    core, y = lax.rem(e, 2), e // 2
    mate = {"enc": e + 1 - 2 * core}
    place = y * 2 + m

    def at_place(p):
        y2 = 1 - y if p & 2 else y
        m2 = 1 - m if p & 1 else m
        return y2, m2

    def peer(p):
        y2, m2 = at_place(p)
        return {"enc": y2 * 2 + core, "mp": m2}

    def ctx_of(k):
        return lax.rem(c + k, n)

    def src_of(k):
        return lax.rem(c - k + n, n)

    near = 3 - 2 * (c // 2)
    far = 4 - near
    is_inner = lax.rem((c + 1) // 2, 2)
    is_outer = 1 - is_inner
    inner, outer = is_inner == 1, is_outer == 1
    turns = [0, is_inner * near + is_outer * 2, far, is_inner * 2 + is_outer * near]

    issued = []
    count = [0]

    def alloc(amount):
        count[0] += amount
        return count[0] - amount

    def describe(src, dst, device, send, recv):
        return pltpu.make_async_remote_copy(
            src_ref=src, dst_ref=dst, send_sem=send_sems.at[send], recv_sem=recv_sems.at[recv],
            device_id=device, device_id_type=MESH,
        )

    def rcopy(src, dst, device):
        i = alloc(1)
        d = describe(src, dst, device, i, i)
        d.start()
        issued.append((None, d))
        return d

    def gather_start(src, buf, base, part=slice(None)):
        def one(k):
            return describe(src, buf.at[c, part], {"ctx": ctx_of(k)}, base + k - 1, base + k - 1)

        last = one(near)
        for d in (one(2), one(far)):
            d.start()
            issued.append((None, d))

        @pl.when(inner)
        def _():
            last.start()

        issued.append((inner, last))

    def gather_wait(buf, base, k, part=slice(None)):
        block = buf.at[c, part]
        describe(block, block, {"ctx": ctx_of(1)}, base, base + k - 1).wait_recv()

    def gather_relay(buf, base, part=slice(None)):
        block = buf.at[src_of(2), part]
        d = describe(block, block, {"ctx": (c - 1) * 3}, base + 3, base + 2 * is_inner * (c - 1))
        issued.append((inner, d))

        @pl.when(inner)
        def _():
            d.start()

    def scatter_send(turn, send, part, relay, base):
        k = turns[turn]
        s = src_of(k)
        at = base + turn - 1
        direct = describe(send.at[s], part.at[k - 1], {"ctx": s}, at, base + k - 1)
        via = describe(send.at[s], relay, {"ctx": 1 + c // 3}, at, base + 3)
        if turn == 2:
            @pl.when(outer)
            def _():
                via.start()

            @pl.when(inner)
            def _():
                direct.start()
        elif turn == 3:
            pl.when(outer)(direct.start)
        else:
            direct.start()
        issued.append((None, direct))

    def scatter_merge(send, part, relay, base):
        k = turns[3]
        s = src_of(k)
        direct = describe(send.at[s], part.at[k - 1], {"ctx": s}, base + 2, base + k - 1)
        via = describe(send.at[s], relay, {"ctx": 1 + c // 3}, base + 2, base + 3)

        @pl.when(inner)
        def _():
            via.wait_recv()
            send[s] = (send[s].astype(F32) + relay[...].astype(F32)).astype(BF16)
            direct.start()

    def scatter_wait(part, base):
        def one(k):
            block = part.at[0]
            describe(block, block, {"ctx": ctx_of(1)}, base, base + k - 1).wait_recv()

        one(2)
        one(far)

        @pl.when(inner)
        def _():
            one(near)

        @pl.when(outer)
        def _():
            part[near - 1] = jnp.zeros(part.shape[1:], BF16)

    barrier = pltpu.get_barrier_semaphore()
    friends = [{"ctx": ctx_of(k)} for k in range(1, n)]
    friends += [{"enc": lax.rem(e + k, n_enc)} for k in range(1, n_enc)]
    friends += [peer(1), peer(3)]
    for f in friends:
        pl.semaphore_signal(barrier, inc=1, device_id=f, device_id_type=MESH)
    pl.semaphore_wait(barrier, len(friends))

    my_rows = pl.ds(pl.multiple_of(core * half + place * rows, rows), rows)
    my_half = pl.ds(pl.multiple_of(core * half, half), half)
    mate_half = pl.ds(pl.multiple_of((1 - core) * half, half), half)
    my_shard = pl.ds(pl.multiple_of(c * shard, shard), shard)

    a1 = alloc(3)
    for k in range(1, n):
        t = ctx_of(k)
        there = pl.ds(pl.multiple_of(t * shard, shard), shard)
        d = describe(
            hid_in.at[my_rows, there], hid_all.at[c, my_rows, :], {"ctx": t}, a1 + k - 1, a1 + k - 1
        )
        d.start()
        issued.append((None, d))
    nearest = {1: near, 2: is_inner * far + is_outer * 2, 3: is_inner * 2 + is_outer * far}
    def fetch(i, src, dst):
        d = pltpu.make_async_copy(src, dst, local_sems.at[i])
        d.start()
        return d

    got_shard = fetch(0, hid_in.at[:, my_shard], hid_all.at[c])
    got_wq = fetch(1, wq_in, wq)
    got_hid = fetch(2, hid_in, hid)
    got_nbr = fetch(3, nbr.at[e], nbr_all.at[pl.ds(e * slots, slots)])
    got_wco = fetch(4, wco_in, wco)
    got_wqkv = fetch(5, wqkv_in, wqkv)
    got_wso = fetch(6, wso, wso_all.at[c])
    nb = []
    for k in range(1, n_enc):
        f = lax.rem(e + k, n_enc)
        nb.append(rcopy(nbr.at[f], nbr_all.at[pl.ds(e * slots, slots)], {"enc": f}))
    gain0 = gains[0:1, my_shard]
    gain1 = gains[1:2, my_shard]

    def project_query(s):
        x = (hid_all[s].astype(F32) * gain0).astype(BF16)
        qsend[s] = dot(x, wq[...]).astype(BF16)

    a2 = {}
    for k in range(1, n):
        s = src_of(nearest[k])
        gather_wait(hid_all, a1, nearest[k], my_rows)
        for p in (3, 1, 2):
            block = hid_all.at[s, my_rows, :]
            a2[k, p] = rcopy(block, block, peer(p))
    ws = (alloc(4), alloc(4))
    deep = feats // 2
    gather_start(wso.at[0:deep], wso_all, ws[0], pl.ds(0, deep))
    got_shard.wait()
    got_wq.wait()
    project_query(c)
    got_hid.wait()
    squares = jnp.zeros((tok, 1), F32)
    for j in range(n):
        x = hid[:, j * shard:(j + 1) * shard].astype(F32)
        squares = squares + jnp.sum(x * x, axis=1, keepdims=True)
    rs0[...] = jnp.broadcast_to(lax.rsqrt(squares / width + epsilon), rs0.shape)
    a3 = {}
    for k in range(1, n):
        s = src_of(nearest[k])
        for p in (1, 2, 3):
            a2[k, p].wait_recv()
        block = hid_all.at[s, my_half, :]
        a3[k] = rcopy(block, block, mate)
    qs = alloc(3)
    for j in range(1, n):
        k = nearest[j]
        s = src_of(k)
        a3[j].wait_recv()
        project_query(s)
        d = describe(qsend.at[s], qpart.at[k - 1], {"ctx": s}, qs + j - 1, qs + k - 1)
        d.start()
        issued.append((None, d))
    got_nbr.wait()
    for d in nb:
        d.wait_recv()
    for k in range(1, n):
        gather_wait(qsend, qs, k)
    q = qsend[c].astype(F32)
    for k in range(n - 1):
        q = q + qpart[k].astype(F32)
    q = (q * rs0[:, 0:1]).astype(BF16)

    per_span, spans = nsrc.shape
    lane = lax.broadcasted_iota(jnp.int32, (SPAN, per_span * SPAN), 1)
    blocks = []
    for i in range(spans):
        kv = []
        for j in range(per_span):
            chosen = nsrc[j, i]
            rank = 0
            for i2 in range(i):
                for j2 in range(per_span):
                    rank = rank + jnp.where(nsrc[j2, i2] == chosen, 1, 0)
            kv.append(nbr_all[chosen * slots + rank])
        blocks.append(jnp.concatenate(kv, axis=0))
    for u in range(heads):
        lo = 2 * u * HD
        sc = []
        for i in range(spans):
            qi = q[i * SPAN:(i + 1) * SPAN, u * HD:(u + 1) * HD]
            si = dot_t(qi, blocks[i][:, lo:lo + HD]) * attn_scale
            sc.append(jnp.where(lane < cnt[i] * SPAN, si, far_below))
        sc = jnp.concatenate(sc, axis=0)
        w = jnp.exp(sc - jnp.max(sc, axis=1, keepdims=True))
        total = jnp.sum(w, axis=1, keepdims=True)
        w = w.astype(BF16)
        mixed = [
            dot(w[i * SPAN:(i + 1) * SPAN], blocks[i][:, lo + HD:lo + 2 * HD])
            for i in range(spans)
        ]
        mixed = jnp.concatenate(mixed, axis=0) / total
        att_all[c, :, u * HD:(u + 1) * HD] = mixed.astype(BF16)

    at = alloc(3)
    for k in range(1, n):
        d = describe(att_all.at[c], att_all.at[c], {"ctx": ctx_of(k)}, at + k - 1, at + k - 1)
        d.start()
        issued.append((None, d))
    gather_start(wso.at[deep:], wso_all, ws[1], pl.ds(deep, deep))

    @pl.when(inner)
    def _():
        gather_wait(wso_all, ws[0], 2, pl.ds(0, deep))

    gather_relay(wso_all, ws[0], pl.ds(0, deep))
    got_wco.wait()
    got_wqkv.wait()

    c2, c3, c4, c5, ssp = {}, {}, {}, {}, []
    kvb, q2b = alloc(4), alloc(4)

    def project_out(j):
        s = src_of(turns[j])
        if j:
            gather_wait(att_all, at, turns[j])
        term[s] = dot(att_all[s], wco[...]).astype(BF16)
        c2[j] = rcopy(term.at[s, mate_half, :], corebuf.at[s], mate)

    def pair_sum(j):
        s = src_of(turns[j])
        c2[j].wait_recv()
        cs[s] = (term[s, my_half, :].astype(F32) + corebuf[s].astype(F32)).astype(BF16)
        for p in (3, 1, 2):
            y2, m2 = at_place(p)
            theirs = pl.ds(pl.multiple_of((y2 * 2 + m2) * rows, rows), rows)
            c3[j, p] = rcopy(cs.at[s, theirs, :], rsbuf.at[p - 1, s], peer(p))

    def plane_sum(j):
        s = src_of(turns[j])
        total = hid_all[s, my_rows, :].astype(F32)
        total = total + cs[s, pl.ds(pl.multiple_of(place * rows, rows), rows), :].astype(F32)
        for p in (1, 2, 3):
            c3[j, p].wait_recv()
            total = total + rsbuf[p - 1, s].astype(F32)
        mid_all[s, my_rows, :] = total.astype(BF16)
        block = mid_all.at[s, my_rows, :]
        for p in (3, 1, 2):
            c4[j, p] = rcopy(block, block, peer(p))

    def plane_share(j):
        s = src_of(turns[j])
        for p in (1, 2, 3):
            c4[j, p].wait_recv()
        block = mid_all.at[s, my_half, :]
        c5[j] = rcopy(block, block, mate)

    def project_kv(j):
        s = src_of(turns[j])
        c5[j].wait_recv()
        x = mid_all[s].astype(F32)
        squares = jnp.sum(x * x, axis=1, keepdims=True)
        sssend[s] = jnp.broadcast_to(squares, (tok, HD)).T[0:8]
        x = (x * gain1).astype(BF16)
        kvsend[s, :, 0:feats] = dot(x, wqkv[1]).astype(BF16)
        kvsend[s, :, feats:] = dot(x, wqkv[2]).astype(BF16)
        if j:
            scatter_send(j, kvsend, kvpart, kvrelay, kvb)
        if j == 3:
            scatter_merge(kvsend, kvpart, kvrelay, kvb)

    stages = (project_out, pair_sum, plane_sum, plane_share, project_kv)
    for step in range(n + len(stages) - 1):
        for i in reversed(range(len(stages))):
            if 0 <= step - i < n:
                stages[i](step - i)
    for k in range(1, n):
        s = src_of(k)
        ssp.append(rcopy(sssend.at[s], sspart.at[k - 1], {"ctx": s}))
    for j in (1, 2, 3, 0):
        s = src_of(turns[j])
        x = (mid_all[s].astype(F32) * gain1).astype(BF16)
        q2send[s] = dot(x, wqkv[0]).astype(BF16)
        if j:
            scatter_send(j, q2send, q2part, q2relay, q2b)
    @pl.when(inner)
    def _():
        gather_wait(wso_all, ws[1], 2, pl.ds(deep, deep))

    gather_relay(wso_all, ws[1], pl.ds(deep, deep))

    my_cols = pl.ds(pl.multiple_of(m * cols, cols), cols)

    def whole(send, part):
        total = send[c].astype(F32)
        for k in range(n - 1):
            total = total + part[k].astype(F32)
        return (total * row_scale).astype(BF16)

    for d in ssp:
        d.wait_recv()
    squares = sssend[c]
    for k in range(n - 1):
        squares = squares + sspart[k]
    squares = jnp.broadcast_to(squares[0:1], (HD, tok)).T[:, 0:1]
    row_scale = lax.rsqrt(squares / width + epsilon)
    scatter_wait(kvpart, kvb)
    kv_all[c] = whole(kvsend, kvpart)
    kvg = alloc(4)
    gather_start(kv_all.at[c], kv_all, kvg)

    scatter_merge(q2send, q2part, q2relay, q2b)


    scatter_wait(q2part, q2b)
    qbuf[...] = whole(q2send, q2part)

    resid = alloc(3)
    residual = []

    def send_residual():
        for k in range(1, n):
            t = ctx_of(k)
            residual.append(
                describe(mid_all.at[t, :, my_cols], midown, {"ctx": t}, resid + k - 1, resid)
            )

        @pl.when(c == e)
        def _():
            for d in residual:
                d.start()
            midown[...] = mid_all[c, :, my_cols]

    def places(s, shape, axis):
        index = lax.broadcasted_iota(jnp.int32, shape, axis)
        first = s * (tok // SPAN)
        found = jnp.zeros(shape, jnp.int32)
        for b in range(tok // SPAN):
            found = jnp.where(index // SPAN == b, order[first + b], found)
        return found * SPAN + lax.rem(index, SPAN)

    query_places = places(c, (tok, 1), 0)
    tops = [jnp.full((tok, 1), far_below, F32) for _ in range(heads)]
    sums = [jnp.zeros((tok, 1), F32) for _ in range(heads)]
    accs = [jnp.zeros((tok, HD), F32) for _ in range(heads)]
    arrivals = (0, is_inner * 2 + is_outer * near, is_inner * near + is_outer * 2, far)
    for i, k in enumerate(arrivals):
        s = src_of(k)
        if i:
            gather_wait(kv_all, kvg, k)
        if i == 1:
            gather_relay(kv_all, kvg)
        if i == n - 1:
            send_residual()
        visible = places(s, (1, tok), 1) <= query_places
        for u in range(heads):
            keys = kv_all[s, :, u * HD:(u + 1) * HD]
            values = kv_all[s, :, feats + u * HD:feats + (u + 1) * HD]
            sc = dot_t(qbuf[:, u * HD:(u + 1) * HD], keys) * attn_scale
            sc = jnp.where(visible, sc, far_below)
            top = jnp.maximum(tops[u], jnp.max(sc, axis=1, keepdims=True))
            w = jnp.where(visible, jnp.exp(sc - top), 0.0)
            shrink = jnp.exp(tops[u] - top)
            sums[u] = sums[u] * shrink + jnp.sum(w, axis=1, keepdims=True)
            accs[u] = accs[u] * shrink + dot(w.astype(BF16), values)
            tops[u] = top
    for u in range(heads):
        att2[:, u * HD:(u + 1) * HD] = (accs[u] / sums[u]).astype(BF16)

    got_wso.wait()
    for i in range(2):
        part = pl.ds(i * deep, deep)
        gather_wait(wso_all, ws[i], near, part)
        gather_wait(wso_all, ws[i], far, part)

        @pl.when(outer)
        def _():
            gather_wait(wso_all, ws[i], 2, part)

    f1, f2 = {}, {}

    def out_term(p, which):
        y2, m2 = at_place(p)
        there = pl.ds(pl.multiple_of(m2 * cols, cols), cols)
        return dot(att2[...], wso_all[y2 * 2 + which, :, there])

    def to_mate(p):
        fother[p] = out_term(p, 1 - core).astype(BF16)
        f1[p] = rcopy(fother.at[p], fcore.at[p], mate)

    for p in (3, 1, 2):
        to_mate(p)
    for p in (3, 1, 2):
        mine = out_term(p, core)
        f1[p].wait_recv()
        fsum[p - 1] = (mine + fcore[p].astype(F32)).astype(BF16)
        f2[p] = rcopy(fsum.at[p - 1], frs.at[p - 1], peer(p))
    to_mate(0)
    mine = out_term(0, core)
    f1[0].wait_recv()

    @pl.when(c == e)
    def _():
        for d in residual:
            d.wait_send()

    @pl.when(c != e)
    def _():
        residual[0].wait_recv()

    total = midown[...].astype(F32) + mine + fcore[0].astype(F32)
    for p in (1, 2, 3):
        f2[p].wait_recv()
        total = total + frs[p - 1].astype(F32)
    out[...] = total.astype(BF16)
    for condition, d in issued:
        if condition is None:
            d.wait_send()
        else:
            pl.when(condition)(d.wait_send)


def scratch_shapes(n, n_enc, tok, width, feats, slots, nbr_rows, pair_width, cols):
    shard = width // n
    half, rows = tok // 2, tok // 8
    return [
        ((tok, width), BF16),
        ((shard, feats), BF16),
        ((feats, shard), BF16),
        ((3, shard, feats), BF16),
        ((n, tok, shard), BF16),
        ((n_enc * slots, nbr_rows, pair_width), BF16),
        ((n, tok, feats), BF16),
        ((n - 1, tok, feats), BF16),
        ((tok, HD), F32),
        ((n, tok, feats), BF16),
        ((n, feats, shard), BF16),
        ((n, tok, shard), BF16),
        ((n, half, shard), BF16),
        ((n, half, shard), BF16),
        ((3, n, rows, shard), BF16),
        ((n, tok, shard), BF16),
        ((n, 8, tok), F32),
        ((n - 1, 8, tok), F32),
        ((n, tok, 2 * feats), BF16),
        ((n - 1, tok, 2 * feats), BF16),
        ((tok, 2 * feats), BF16),
        ((n, tok, feats), BF16),
        ((n - 1, tok, feats), BF16),
        ((tok, feats), BF16),
        ((tok, feats), BF16),
        ((n, tok, 2 * feats), BF16),
        ((tok, cols), BF16),
        ((tok, feats), BF16),
        ((4, tok, cols), BF16),
        ((4, tok, cols), BF16),
        ((3, tok, cols), BF16),
        ((3, tok, cols), BF16),
    ]


def per_device_any(sizes, *args):
    n, n_enc, n_mp = sizes
    hidden_in, norm_gains, w_cross_query, w_cross_out, w_self_qkv, w_self_out, nbr_kv = args[:7]
    tok, width = hidden_in.shape
    feats = w_cross_query.shape[1]
    cols = width // (n_enc * n_mp)
    slots, nbr_rows, pair_width = nbr_kv.shape[3:]
    held = scratch_shapes(n, n_enc, tok, width, feats, slots, nbr_rows, pair_width, cols)
    need = sum(math.prod(shape) * jnp.dtype(kind).itemsize for shape, kind in held)
    if need > VMEM_GRANT // 2 or sizes != (4, 4, 2) or width != n * 2 * cols:
        return per_device(*args)
    copies = 128
    vmem = pl.BlockSpec(memory_space=pltpu.VMEM)
    smem = pl.BlockSpec(memory_space=pltpu.SMEM)
    hbm = pl.BlockSpec(memory_space=pl.ANY)
    return pl.pallas_call(
        block_kernel,
        out_shape=jax.ShapeDtypeStruct((tok, cols), BF16),
        in_specs=[hbm, vmem, hbm, hbm, hbm, hbm, hbm] + [smem] * 3,
        out_specs=vmem,
        scratch_shapes=[pltpu.VMEM(shape, kind) for shape, kind in held]
        + [pltpu.SemaphoreType.DMA((copies,)), pltpu.SemaphoreType.DMA((copies,))]
        + [pltpu.SemaphoreType.DMA((8,))],
        compiler_params=pltpu.CompilerParams(
            collective_id=0, has_side_effects=True, vmem_limit_bytes=VMEM_GRANT
        ),
    )(
        hidden_in, norm_gains, w_cross_query, w_cross_out,
        jnp.transpose(w_self_qkv, (1, 0, 2)), w_self_out,
        nbr_kv[0, 0], args[7], args[8].T, args[9],
    )


def solution(mesh):
    in_specs = (
        P("ctx", None),
        P(),
        P("ctx", ("enc", "mp")),
        P(("enc", "mp"), "ctx"),
        P("ctx", None, ("enc", "mp")),
        P(("enc", "mp"), "ctx"),
        P("ctx", "enc", None, None, None, "mp"),
        P("ctx"),
        P("ctx", None),
        P(),
    )
    out_specs = P("ctx", ("enc", "mp"))
    sizes = (mesh.shape["ctx"], mesh.shape["enc"], mesh.shape["mp"])
    return jax.shard_map(
        functools.partial(per_device_any, sizes), mesh=mesh, in_specs=in_specs, out_specs=out_specs, check_vma=False
    )
```

```python
import functools
import math

import jax
import jax.numpy as jnp
from jax import lax
from jax.experimental import pallas as pl
from jax.experimental.pallas import tpu as pltpu
from jax.sharding import PartitionSpec as P

MESH = pl.DeviceIdType.MESH
VMEM_GRANT = 56 * 1024 * 1024
BF16 = jnp.bfloat16
F32 = jnp.float32

HD = 128
SPAN = 64


epsilon = 1e-05
far_below = -1e30


def rms_rows(row_values, gain_row):
    values = row_values.astype(jnp.float32)
    row_scale = lax.rsqrt(jnp.mean(values * values, axis=-1, keepdims=True) + epsilon)
    return (values * row_scale * gain_row).astype(jnp.bfloat16)


def token_places(order_table, first_row, row_count):
    tokens = first_row + jnp.arange(row_count, dtype=jnp.int32)
    blocks = tokens // SPAN
    matches = blocks[:, None] == jnp.arange(order_table.shape[0], dtype=jnp.int32)[None, :]
    placed = jnp.sum(jnp.where(matches, order_table[None, :], 0), axis=1)
    return placed * SPAN + tokens % SPAN


def per_device(
    hidden_in,
    norm_gains,
    w_cross_query,
    w_cross_out,
    w_self_qkv,
    w_self_out,
    nbr_kv,
    nbr_count,
    nbr_source,
    span_order,
):
    tok_rows, model_width = hidden_in.shape
    features = w_cross_query.shape[1]
    heads_here = features // HD
    groups = lax.axis_size(("enc", "mp"))
    share_width = model_width // groups
    group_index = lax.axis_index(("enc", "mp"))
    column = lax.axis_index("ctx")
    attn_scale = 1.0 / math.sqrt(HD)
    normed = rms_rows(hidden_in, norm_gains[0])
    columns_part = normed
    cross_query = jnp.dot(
        columns_part,
        lax.all_gather(w_cross_query, "ctx", axis=0, tiled=True),
        preferred_element_type=jnp.float32,
    ).astype(jnp.bfloat16)
    arrived = lax.all_to_all(nbr_kv[0, 0], "enc", split_axis=0, concat_axis=0, tiled=True)
    sources, slot_count, nbr_rows, pair_width = arrived.shape
    flattened = arrived.reshape(sources * slot_count, nbr_rows, pair_width)
    spans_here, per_span = nbr_source.shape
    chosen = nbr_source.reshape(-1)
    matches = (chosen[:, None] == jnp.arange(sources, dtype=jnp.int32)[None, :]).astype(jnp.int32)
    earlier = jnp.cumsum(matches, axis=0) - matches
    places = chosen * slot_count + jnp.sum(earlier * matches, axis=1)
    picked = jnp.take(flattened, places, axis=0)
    picked = picked.reshape(spans_here, per_span, nbr_rows, heads_here, 2, HD)
    nbr_keys = picked[:, :, :, :, 0, :]
    nbr_values = picked[:, :, :, :, 1, :]
    queries = cross_query.reshape(spans_here, tok_rows // spans_here, heads_here, HD)
    scores = (
        jnp.einsum("cqhd,cjrhd->chqjr", queries, nbr_keys, preferred_element_type=jnp.float32)
        * attn_scale
    )
    alive_mask = jnp.arange(per_span, dtype=jnp.int32)[None, :] < nbr_count[:, None]
    scores = jnp.where(alive_mask[:, None, None, :, None], scores, far_below)
    row_top = jnp.max(scores, axis=(3, 4), keepdims=True)
    weights_f = jnp.exp(scores - row_top)
    row_total = jnp.sum(weights_f, axis=(3, 4))
    mixed_heads = (
        jnp.einsum(
            "chqjr,cjrhd->chqd",
            weights_f.astype(jnp.bfloat16),
            nbr_values,
            preferred_element_type=jnp.float32,
        )
        / row_total[..., None]
    )
    cross_att = mixed_heads.transpose(0, 2, 1, 3).reshape(tok_rows, features).astype(jnp.bfloat16)
    cross_term = jnp.dot(
        cross_att,
        lax.all_gather(w_cross_out, "ctx", axis=1, tiled=True),
        preferred_element_type=jnp.float32,
    )
    summed = lax.psum(cross_term.astype(jnp.bfloat16), ("enc", "mp")).astype(jnp.float32)
    mid_full = (hidden_in.astype(jnp.float32) + summed).astype(jnp.bfloat16)
    mid_normed = rms_rows(mid_full, norm_gains[1])
    mid_share = lax.dynamic_slice_in_dim(mid_full, group_index * share_width, share_width, 1)
    shard_piece = lax.all_gather(w_self_qkv, "ctx", axis=0, tiled=True)
    columns_part = mid_normed
    projected = jnp.dot(
        columns_part,
        shard_piece.reshape(shard_piece.shape[0], 3 * features),
        preferred_element_type=jnp.float32,
    )
    projected = projected.astype(jnp.bfloat16).reshape(tok_rows, 3, heads_here, HD)
    self_query = projected[:, 0]
    keys_values = projected[:, 1:]
    query_places = token_places(span_order, column * tok_rows, tok_rows)
    shard_piece = lax.all_gather(keys_values, "ctx", axis=0, tiled=True)
    old_top = jnp.full((heads_here, tok_rows), far_below, jnp.float32)
    key_places = token_places(span_order, jnp.int32(0), shard_piece.shape[0])
    block_scores = (
        jnp.einsum(
            "qhd,khd->hqk", self_query, shard_piece[:, 0], preferred_element_type=jnp.float32
        )
        * attn_scale
    )
    visible = key_places[None, None, :] <= query_places[None, :, None]
    block_scores = jnp.where(visible, block_scores, far_below)
    new_top = jnp.maximum(old_top, jnp.max(block_scores, axis=2))
    block_weights = jnp.where(visible, jnp.exp(block_scores - new_top[..., None]), 0.0)
    new_total = jnp.sum(block_weights, axis=2)
    running = jnp.einsum(
        "hqk,khd->hqd",
        block_weights.astype(jnp.bfloat16),
        shard_piece[:, 1],
        preferred_element_type=jnp.float32,
    )
    self_att = (
        (running / new_total[..., None])
        .transpose(1, 0, 2)
        .reshape(tok_rows, features)
        .astype(jnp.bfloat16)
    )
    self_term = jnp.dot(
        self_att,
        lax.all_gather(w_self_out, "ctx", axis=1, tiled=True),
        preferred_element_type=jnp.float32,
    )
    out_share = lax.psum_scatter(
        self_term.astype(jnp.bfloat16), ("enc", "mp"), scatter_dimension=1, tiled=True
    ).astype(jnp.float32)
    return (mid_share.astype(jnp.float32) + out_share).astype(jnp.bfloat16)


def dot(a, b):
    return jnp.dot(a, b, preferred_element_type=F32)


def dot_t(a, b):
    return lax.dot_general(a, b, (((1,), (1,)), ((), ())), preferred_element_type=F32)


def block_kernel(
    hid_in, gains, wq_in, wco_in, wqkv_in, wso, nbr, cnt, nsrc, order, out,
    hid, wq, wco, wqkv, hid_all, nbr_all, qsend, qpart, qrelay, rs0, att_all, wso_all, term, corebuf, cs, rsbuf, mid_all,
    sssend, sspart, kvsend, kvpart, kvrelay, q2send, q2part, q2relay, qbuf, kv_all, midown, att2, fother, fcore, fsum, frs,
    send_sems, recv_sems, local_sems,
):
    c, e, m = lax.axis_index("ctx"), lax.axis_index("enc"), lax.axis_index("mp")
    n = hid_all.shape[0]
    tok, width = hid.shape
    shard = width // n
    feats = wq.shape[1]
    heads = feats // HD
    slots = nbr.shape[1]
    n_enc = nbr.shape[0]
    rows = tok // 8
    half = tok // 2
    cols = out.shape[1]
    attn_scale = 1.0 / math.sqrt(HD)

    core, y = lax.rem(e, 2), e // 2
    mate = {"enc": e + 1 - 2 * core}
    place = y * 2 + m

    def at_place(p):
        y2 = 1 - y if p & 2 else y
        m2 = 1 - m if p & 1 else m
        return y2, m2

    def peer(p):
        y2, m2 = at_place(p)
        return {"enc": y2 * 2 + core, "mp": m2}

    def ctx_of(k):
        return lax.rem(c + k, n)

    def src_of(k):
        return lax.rem(c - k + n, n)

    near = 3 - 2 * (c // 2)
    far = 4 - near
    is_inner = lax.rem((c + 1) // 2, 2)
    is_outer = 1 - is_inner
    inner, outer = is_inner == 1, is_outer == 1
    turns = [0, is_inner * near + is_outer * 2, far, is_inner * 2 + is_outer * near]

    issued = []
    count = [0]

    def alloc(amount):
        count[0] += amount
        return count[0] - amount

    def describe(src, dst, device, send, recv):
        return pltpu.make_async_remote_copy(
            src_ref=src, dst_ref=dst, send_sem=send_sems.at[send], recv_sem=recv_sems.at[recv],
            device_id=device, device_id_type=MESH,
        )

    def rcopy(src, dst, device):
        i = alloc(1)
        d = describe(src, dst, device, i, i)
        d.start()
        issued.append((None, d))
        return d

    def gather_start(src, buf, base, part=slice(None)):
        def one(k):
            return describe(src, buf.at[c, part], {"ctx": ctx_of(k)}, base + k - 1, base + k - 1)

        last = one(near)
        for d in (one(2), one(far)):
            d.start()
            issued.append((None, d))

        @pl.when(inner)
        def _():
            last.start()

        issued.append((inner, last))

    def gather_wait(buf, base, k, part=slice(None)):
        block = buf.at[c, part]
        describe(block, block, {"ctx": ctx_of(1)}, base, base + k - 1).wait_recv()

    def gather_relay(buf, base, part=slice(None)):
        block = buf.at[src_of(2), part]
        d = describe(block, block, {"ctx": (c - 1) * 3}, base + 3, base + 2 * is_inner * (c - 1))
        issued.append((inner, d))

        @pl.when(inner)
        def _():
            d.start()

    def scatter_send(turn, send, part, relay, base):
        k = turns[turn]
        s = src_of(k)
        at = base + turn - 1
        direct = describe(send.at[s], part.at[k - 1], {"ctx": s}, at, base + k - 1)
        via = describe(send.at[s], relay, {"ctx": 1 + c // 3}, at, base + 3)
        if turn == 2:
            @pl.when(outer)
            def _():
                via.start()

            @pl.when(inner)
            def _():
                direct.start()
        elif turn == 3:
            pl.when(outer)(direct.start)
        else:
            direct.start()
        issued.append((None, direct))

    def scatter_merge(send, part, relay, base):
        k = turns[3]
        s = src_of(k)
        direct = describe(send.at[s], part.at[k - 1], {"ctx": s}, base + 2, base + k - 1)
        via = describe(send.at[s], relay, {"ctx": 1 + c // 3}, base + 2, base + 3)

        @pl.when(inner)
        def _():
            via.wait_recv()
            send[s] = (send[s].astype(F32) + relay[...].astype(F32)).astype(BF16)
            direct.start()

    def scatter_wait(part, base):
        def one(k):
            block = part.at[0]
            describe(block, block, {"ctx": ctx_of(1)}, base, base + k - 1).wait_recv()

        one(2)
        one(far)

        @pl.when(inner)
        def _():
            one(near)

        @pl.when(outer)
        def _():
            part[near - 1] = jnp.zeros(part.shape[1:], BF16)

    barrier = pltpu.get_barrier_semaphore()
    friends = [{"ctx": ctx_of(k)} for k in range(1, n)]
    friends += [{"enc": lax.rem(e + k, n_enc)} for k in range(1, n_enc)]
    friends += [peer(1), peer(3)]
    for f in friends:
        pl.semaphore_signal(barrier, inc=1, device_id=f, device_id_type=MESH)
    pl.semaphore_wait(barrier, len(friends))

    my_rows = pl.ds(pl.multiple_of(core * half + place * rows, rows), rows)
    my_half = pl.ds(pl.multiple_of(core * half, half), half)
    mate_half = pl.ds(pl.multiple_of((1 - core) * half, half), half)
    my_shard = pl.ds(pl.multiple_of(c * shard, shard), shard)

    a1 = alloc(3)
    for k in range(1, n):
        t = ctx_of(k)
        there = pl.ds(pl.multiple_of(t * shard, shard), shard)
        d = describe(
            hid_in.at[my_rows, there], hid_all.at[c, my_rows, :], {"ctx": t}, a1 + k - 1, a1 + k - 1
        )
        d.start()
        issued.append((None, d))
    def fetch(i, src, dst):
        d = pltpu.make_async_copy(src, dst, local_sems.at[i])
        d.start()
        return d

    got_shard = fetch(0, hid_in.at[:, my_shard], hid_all.at[c])
    got_wq = fetch(1, wq_in, wq)
    got_hid = fetch(2, hid_in, hid)
    got_nbr = fetch(3, nbr.at[e], nbr_all.at[pl.ds(e * slots, slots)])
    got_wco = fetch(4, wco_in, wco)
    got_wqkv = fetch(5, wqkv_in, wqkv)
    got_wso = fetch(6, wso, wso_all.at[c])
    nb = []
    for k in range(1, n_enc):
        f = lax.rem(e + k, n_enc)
        nb.append(rcopy(nbr.at[f], nbr_all.at[pl.ds(e * slots, slots)], {"enc": f}))
    gain0 = gains[0:1, my_shard]
    gain1 = gains[1:2, my_shard]

    def project_query(s):
        x = (hid_all[s].astype(F32) * gain0).astype(BF16)
        qsend[s] = dot(x, wq[...]).astype(BF16)

    a2 = {}
    for k in range(1, n):
        s = src_of(turns[k])
        gather_wait(hid_all, a1, turns[k], my_rows)
        for p in (3, 1, 2):
            block = hid_all.at[s, my_rows, :]
            a2[k, p] = rcopy(block, block, peer(p))
    ws = (alloc(4), alloc(4))
    deep = feats // 2
    gather_start(wso.at[0:deep], wso_all, ws[0], pl.ds(0, deep))
    got_shard.wait()
    got_wq.wait()
    project_query(c)
    got_hid.wait()
    squares = jnp.zeros((tok, 1), F32)
    for j in range(n):
        x = hid[:, j * shard:(j + 1) * shard].astype(F32)
        squares = squares + jnp.sum(x * x, axis=1, keepdims=True)
    rs0[...] = jnp.broadcast_to(lax.rsqrt(squares / width + epsilon), rs0.shape)
    a3 = {}
    for k in range(1, n):
        s = src_of(turns[k])
        for p in (1, 2, 3):
            a2[k, p].wait_recv()
        block = hid_all.at[s, my_half, :]
        a3[k] = rcopy(block, block, mate)
    qs = alloc(4)
    for j in range(1, n):
        a3[j].wait_recv()
        project_query(src_of(turns[j]))
        scatter_send(j, qsend, qpart, qrelay, qs)
    scatter_merge(qsend, qpart, qrelay, qs)
    got_nbr.wait()
    for d in nb:
        d.wait_recv()
    scatter_wait(qpart, qs)
    q = qsend[c].astype(F32)
    for k in range(n - 1):
        q = q + qpart[k].astype(F32)
    q = (q * rs0[:, 0:1]).astype(BF16)

    per_span, spans = nsrc.shape
    lane = lax.broadcasted_iota(jnp.int32, (SPAN, per_span * SPAN), 1)
    blocks = []
    for i in range(spans):
        kv = []
        for j in range(per_span):
            chosen = nsrc[j, i]
            rank = 0
            for i2 in range(i):
                for j2 in range(per_span):
                    rank = rank + jnp.where(nsrc[j2, i2] == chosen, 1, 0)
            kv.append(nbr_all[chosen * slots + rank])
        blocks.append(jnp.concatenate(kv, axis=0))
    for u in range(heads):
        lo = 2 * u * HD
        sc = []
        for i in range(spans):
            qi = q[i * SPAN:(i + 1) * SPAN, u * HD:(u + 1) * HD]
            si = dot_t(qi, blocks[i][:, lo:lo + HD]) * attn_scale
            sc.append(jnp.where(lane < cnt[i] * SPAN, si, far_below))
        sc = jnp.concatenate(sc, axis=0)
        w = jnp.exp(sc - jnp.max(sc, axis=1, keepdims=True))
        total = jnp.sum(w, axis=1, keepdims=True)
        w = w.astype(BF16)
        mixed = [
            dot(w[i * SPAN:(i + 1) * SPAN], blocks[i][:, lo + HD:lo + 2 * HD])
            for i in range(spans)
        ]
        mixed = jnp.concatenate(mixed, axis=0) / total
        att_all[c, :, u * HD:(u + 1) * HD] = mixed.astype(BF16)

    at = alloc(4)
    gather_start(att_all.at[c], att_all, at)
    gather_start(wso.at[deep:], wso_all, ws[1], pl.ds(deep, deep))

    @pl.when(inner)
    def _():
        gather_wait(wso_all, ws[0], 2, pl.ds(0, deep))

    gather_relay(wso_all, ws[0], pl.ds(0, deep))
    got_wco.wait()
    got_wqkv.wait()

    c2, c3, c4, c5, ssp = {}, {}, {}, {}, []
    kvb, q2b = alloc(4), alloc(4)

    def project_out(j):
        s = src_of(turns[j])
        if j == n - 1:
            pl.when(outer)(lambda: gather_wait(att_all, at, near))
        elif j:
            gather_wait(att_all, at, turns[j])
        term[s] = dot(att_all[s], wco[...]).astype(BF16)
        c2[j] = rcopy(term.at[s, mate_half, :], corebuf.at[s], mate)

    def pair_sum(j):
        s = src_of(turns[j])
        c2[j].wait_recv()
        cs[s] = (term[s, my_half, :].astype(F32) + corebuf[s].astype(F32)).astype(BF16)
        for p in (3, 1, 2):
            y2, m2 = at_place(p)
            theirs = pl.ds(pl.multiple_of((y2 * 2 + m2) * rows, rows), rows)
            c3[j, p] = rcopy(cs.at[s, theirs, :], rsbuf.at[p - 1, s], peer(p))

    def plane_sum(j):
        s = src_of(turns[j])
        total = hid_all[s, my_rows, :].astype(F32)
        total = total + cs[s, pl.ds(pl.multiple_of(place * rows, rows), rows), :].astype(F32)
        for p in (1, 2, 3):
            c3[j, p].wait_recv()
            total = total + rsbuf[p - 1, s].astype(F32)
        mid_all[s, my_rows, :] = total.astype(BF16)
        block = mid_all.at[s, my_rows, :]
        for p in (3, 1, 2):
            c4[j, p] = rcopy(block, block, peer(p))

    def plane_share(j):
        s = src_of(turns[j])
        for p in (1, 2, 3):
            c4[j, p].wait_recv()
        block = mid_all.at[s, my_half, :]
        c5[j] = rcopy(block, block, mate)

    def project_kv(j):
        s = src_of(turns[j])
        c5[j].wait_recv()
        x = mid_all[s].astype(F32)
        squares = jnp.sum(x * x, axis=1, keepdims=True)
        sssend[s] = jnp.broadcast_to(squares, (tok, HD)).T[0:8]
        x = (x * gain1).astype(BF16)
        kvsend[s, :, 0:feats] = dot(x, wqkv[1]).astype(BF16)
        kvsend[s, :, feats:] = dot(x, wqkv[2]).astype(BF16)
        if j:
            scatter_send(j, kvsend, kvpart, kvrelay, kvb)
        if j == 3:
            scatter_merge(kvsend, kvpart, kvrelay, kvb)

    stages = (project_out, pair_sum, plane_sum, plane_share, project_kv)
    for step in range(n + len(stages) - 1):
        if step == 2:
            pl.when(inner)(lambda: gather_wait(att_all, at, 2))
            gather_relay(att_all, at)
        for i in reversed(range(len(stages))):
            if 0 <= step - i < n:
                stages[i](step - i)
    for k in range(1, n):
        s = src_of(k)
        ssp.append(rcopy(sssend.at[s], sspart.at[k - 1], {"ctx": s}))
    for j in (1, 2, 3, 0):
        s = src_of(turns[j])
        x = (mid_all[s].astype(F32) * gain1).astype(BF16)
        q2send[s] = dot(x, wqkv[0]).astype(BF16)
        if j:
            scatter_send(j, q2send, q2part, q2relay, q2b)
    @pl.when(inner)
    def _():
        gather_wait(wso_all, ws[1], 2, pl.ds(deep, deep))

    gather_relay(wso_all, ws[1], pl.ds(deep, deep))

    my_cols = pl.ds(pl.multiple_of(m * cols, cols), cols)

    def whole(send, part):
        total = send[c].astype(F32)
        for k in range(n - 1):
            total = total + part[k].astype(F32)
        return (total * row_scale).astype(BF16)

    for d in ssp:
        d.wait_recv()
    squares = sssend[c]
    for k in range(n - 1):
        squares = squares + sspart[k]
    squares = jnp.broadcast_to(squares[0:1], (HD, tok)).T[:, 0:1]
    row_scale = lax.rsqrt(squares / width + epsilon)
    scatter_wait(kvpart, kvb)
    kv_all[c] = whole(kvsend, kvpart)
    kvg = alloc(4)
    gather_start(kv_all.at[c], kv_all, kvg)

    scatter_merge(q2send, q2part, q2relay, q2b)


    scatter_wait(q2part, q2b)
    qbuf[...] = whole(q2send, q2part)

    resid = alloc(3)
    residual = []

    def send_residual():
        for k in range(1, n):
            t = ctx_of(k)
            residual.append(
                describe(mid_all.at[t, :, my_cols], midown, {"ctx": t}, resid + k - 1, resid)
            )

        @pl.when(c == e)
        def _():
            for d in residual:
                d.start()
            midown[...] = mid_all[c, :, my_cols]

    def places(s, shape, axis):
        index = lax.broadcasted_iota(jnp.int32, shape, axis)
        first = s * (tok // SPAN)
        found = jnp.zeros(shape, jnp.int32)
        for b in range(tok // SPAN):
            found = jnp.where(index // SPAN == b, order[first + b], found)
        return found * SPAN + lax.rem(index, SPAN)

    query_places = places(c, (tok, 1), 0)
    tops = [jnp.full((tok, 1), far_below, F32) for _ in range(heads)]
    sums = [jnp.zeros((tok, 1), F32) for _ in range(heads)]
    accs = [jnp.zeros((tok, HD), F32) for _ in range(heads)]
    arrivals = (0, is_inner * 2 + is_outer * near, is_inner * near + is_outer * 2, far)
    for i, k in enumerate(arrivals):
        s = src_of(k)
        if i:
            gather_wait(kv_all, kvg, k)
        if i == 1:
            gather_relay(kv_all, kvg)
        if i == n - 1:
            send_residual()
        visible = places(s, (1, tok), 1) <= query_places
        for u in range(heads):
            keys = kv_all[s, :, u * HD:(u + 1) * HD]
            values = kv_all[s, :, feats + u * HD:feats + (u + 1) * HD]
            sc = dot_t(qbuf[:, u * HD:(u + 1) * HD], keys) * attn_scale
            sc = jnp.where(visible, sc, far_below)
            top = jnp.maximum(tops[u], jnp.max(sc, axis=1, keepdims=True))
            w = jnp.where(visible, jnp.exp(sc - top), 0.0)
            shrink = jnp.exp(tops[u] - top)
            sums[u] = sums[u] * shrink + jnp.sum(w, axis=1, keepdims=True)
            accs[u] = accs[u] * shrink + dot(w.astype(BF16), values)
            tops[u] = top
    for u in range(heads):
        att2[:, u * HD:(u + 1) * HD] = (accs[u] / sums[u]).astype(BF16)

    got_wso.wait()
    for i in range(2):
        part = pl.ds(i * deep, deep)
        gather_wait(wso_all, ws[i], near, part)
        gather_wait(wso_all, ws[i], far, part)

        @pl.when(outer)
        def _():
            gather_wait(wso_all, ws[i], 2, part)

    f1, f2 = {}, {}

    def out_term(p, which):
        y2, m2 = at_place(p)
        there = pl.ds(pl.multiple_of(m2 * cols, cols), cols)
        return dot(att2[...], wso_all[y2 * 2 + which, :, there])

    def to_mate(p):
        fother[p] = out_term(p, 1 - core).astype(BF16)
        f1[p] = rcopy(fother.at[p], fcore.at[p], mate)

    for p in (3, 1, 2):
        to_mate(p)
    for p in (3, 1, 2):
        mine = out_term(p, core)
        f1[p].wait_recv()
        fsum[p - 1] = (mine + fcore[p].astype(F32)).astype(BF16)
        f2[p] = rcopy(fsum.at[p - 1], frs.at[p - 1], peer(p))
    to_mate(0)
    mine = out_term(0, core)
    f1[0].wait_recv()

    @pl.when(c == e)
    def _():
        for d in residual:
            d.wait_send()

    @pl.when(c != e)
    def _():
        residual[0].wait_recv()

    total = midown[...].astype(F32) + mine + fcore[0].astype(F32)
    for p in (1, 2, 3):
        f2[p].wait_recv()
        total = total + frs[p - 1].astype(F32)
    out[...] = total.astype(BF16)
    for condition, d in issued:
        if condition is None:
            d.wait_send()
        else:
            pl.when(condition)(d.wait_send)


def scratch_shapes(n, n_enc, tok, width, feats, slots, nbr_rows, pair_width, cols):
    shard = width // n
    half, rows = tok // 2, tok // 8
    return [
        ((tok, width), BF16),
        ((shard, feats), BF16),
        ((feats, shard), BF16),
        ((3, shard, feats), BF16),
        ((n, tok, shard), BF16),
        ((n_enc * slots, nbr_rows, pair_width), BF16),
        ((n, tok, feats), BF16),
        ((n - 1, tok, feats), BF16),
        ((tok, feats), BF16),
        ((tok, HD), F32),
        ((n, tok, feats), BF16),
        ((n, feats, shard), BF16),
        ((n, tok, shard), BF16),
        ((n, half, shard), BF16),
        ((n, half, shard), BF16),
        ((3, n, rows, shard), BF16),
        ((n, tok, shard), BF16),
        ((n, 8, tok), F32),
        ((n - 1, 8, tok), F32),
        ((n, tok, 2 * feats), BF16),
        ((n - 1, tok, 2 * feats), BF16),
        ((tok, 2 * feats), BF16),
        ((n, tok, feats), BF16),
        ((n - 1, tok, feats), BF16),
        ((tok, feats), BF16),
        ((tok, feats), BF16),
        ((n, tok, 2 * feats), BF16),
        ((tok, cols), BF16),
        ((tok, feats), BF16),
        ((4, tok, cols), BF16),
        ((4, tok, cols), BF16),
        ((3, tok, cols), BF16),
        ((3, tok, cols), BF16),
    ]


def per_device_any(sizes, *args):
    n, n_enc, n_mp = sizes
    hidden_in, norm_gains, w_cross_query, w_cross_out, w_self_qkv, w_self_out, nbr_kv = args[:7]
    tok, width = hidden_in.shape
    feats = w_cross_query.shape[1]
    cols = width // (n_enc * n_mp)
    slots, nbr_rows, pair_width = nbr_kv.shape[3:]
    held = scratch_shapes(n, n_enc, tok, width, feats, slots, nbr_rows, pair_width, cols)
    need = sum(math.prod(shape) * jnp.dtype(kind).itemsize for shape, kind in held)
    if need > VMEM_GRANT // 2 or sizes != (4, 4, 2) or width != n * 2 * cols:
        return per_device(*args)
    copies = 128
    vmem = pl.BlockSpec(memory_space=pltpu.VMEM)
    smem = pl.BlockSpec(memory_space=pltpu.SMEM)
    hbm = pl.BlockSpec(memory_space=pl.ANY)
    return pl.pallas_call(
        block_kernel,
        out_shape=jax.ShapeDtypeStruct((tok, cols), BF16),
        in_specs=[hbm, vmem, hbm, hbm, hbm, hbm, hbm] + [smem] * 3,
        out_specs=vmem,
        scratch_shapes=[pltpu.VMEM(shape, kind) for shape, kind in held]
        + [pltpu.SemaphoreType.DMA((copies,)), pltpu.SemaphoreType.DMA((copies,))]
        + [pltpu.SemaphoreType.DMA((8,))],
        compiler_params=pltpu.CompilerParams(
            collective_id=0, has_side_effects=True, vmem_limit_bytes=VMEM_GRANT
        ),
    )(
        hidden_in, norm_gains, w_cross_query, w_cross_out,
        jnp.transpose(w_self_qkv, (1, 0, 2)), w_self_out,
        nbr_kv[0, 0], args[7], args[8].T, args[9],
    )


def solution(mesh):
    in_specs = (
        P("ctx", None),
        P(),
        P("ctx", ("enc", "mp")),
        P(("enc", "mp"), "ctx"),
        P("ctx", None, ("enc", "mp")),
        P(("enc", "mp"), "ctx"),
        P("ctx", "enc", None, None, None, "mp"),
        P("ctx"),
        P("ctx", None),
        P(),
    )
    out_specs = P("ctx", ("enc", "mp"))
    sizes = (mesh.shape["ctx"], mesh.shape["enc"], mesh.shape["mp"])
    return jax.shard_map(
        functools.partial(per_device_any, sizes), mesh=mesh, in_specs=in_specs, out_specs=out_specs, check_vma=False
    )
```
